256 devices in a mesh: lon: 64 (over x_hi, z, y), lat: 4 (over x_lo, core).
Axes of the slice: x: 4 (x_hi: 2, x_lo: 2; x = x_hi * 2 + x_lo), y: 4, z: 8, core: 2. Of those that a mesh axis runs over, the one named last changes fastest.
Arguments:
- tokens: bfloat16 [4, 24, 768, 1024], P(None, 'lat', 'lon'), may hold values from -6 to 6
- cotangent: bfloat16 [4, 24, 768, 1024], P(None, 'lat', 'lon'), may hold values from -16 to 16
- norm_scale_vector: bfloat16 [1024], replicated, may hold values from 0.099609375 to 1.8984375
- query_matrix: bfloat16 [1024, 1024], replicated, may hold values from -1 to 1
- key_matrix: bfloat16 [1024, 1024], replicated, may hold values from -1 to 1
- value_matrix: bfloat16 [1024, 1024], replicated, may hold values from -0.1875 to 0.1875
- output_matrix: bfloat16 [1024, 1024], replicated, may hold values from -0.1875 to 0.1875
- adapter_down_maps: bfloat16 [4, 1024, 32], replicated, may hold values from -0.1875 to 0.1875
- adapter_up_maps: bfloat16 [4, 32, 1024], replicated, may hold values from -1 to 1
Outputs:
- tokens_grad: bfloat16 [4, 24, 768, 1024], P(None, 'lat', 'lon')
- lora_down_grad: float32 [4096, 32], P(('lon', 'lat'))
- lora_up_grad: float32 [32, 4096], P(None, ('lon', 'lat'))
The draws below stay inside these ranges and needn't reach their ends.
All inputs are finite; a program needn't handle non-finite values.
Results may differ from the reference program's by a relative error of at most 0.015.
The reference program's roundings to bfloat16 on the way count: a program that leaves them out, or rounds other values in their place, can miss the bound.
Values may be sent and summed in bfloat16 or wider, within the bound.
A program may use at most 128 MiB of HBM per device.

```python
import math
import jax
import jax.numpy as jnp
from jax import lax

MODEL_WIDTH = 1024
HEADS = 16
ADAPTER_RANK = 32
LEV = 4
WLEV = 2
WLAT = 6
WLON = 12
NLAT = 24
NLON = 768
TOKENS = 73728


def draw_query_matrix(key, part):
    key = jax.random.fold_in(key, 5)
    own = jax.random.truncated_normal(key, -4.0, 4.0, (MODEL_WIDTH, MODEL_WIDTH), jnp.float32)
    mixed = own / math.sqrt(MODEL_WIDTH)
    return jnp.clip(mixed, -1.0, 1.0).astype(jnp.bfloat16)


def draw_key_matrix(key, part):
    key = jax.random.fold_in(key, 7)
    own = jax.random.truncated_normal(key, -4.0, 4.0, (MODEL_WIDTH, MODEL_WIDTH), jnp.float32)
    mixed = own / math.sqrt(MODEL_WIDTH)
    return jnp.clip(mixed, -1.0, 1.0).astype(jnp.bfloat16)


def with_spikes(entries, key, source, target, shards_of, factor):
    def block_of(dim):
        return (jnp.arange(entries.shape[dim]) // (entries.shape[dim] // shards_of)).reshape((-1,) + (1,) * (entries.ndim - 1 - dim))

    one_side = jax.random.permutation(key, shards_of)[block_of(target)]
    second = (block_of(target) + shards_of // 2) % shards_of
    return jnp.where((block_of(source) == one_side) | (block_of(source) == second), factor * entries, entries)


def block_levels(rng, shape, pieces, low, top_value):
    def one(dim, shards_of):
        steps = jax.random.uniform(jax.random.fold_in(jax.random.fold_in(rng, 6), dim), (shards_of,), jnp.float32, low / len(pieces), top_value / len(pieces))
        return jnp.repeat(jnp.exp(steps), shape[dim] // shards_of).reshape((-1,) + (1,) * (len(shape) - dim - 1))

    loudness = one(*pieces[0])
    for cut in pieces[1:]:
        loudness = loudness * one(*cut)
    return loudness


def noise(own_key, shape, deviation, most, shards=(), kind=jnp.bfloat16):
    result = jax.random.normal(own_key, shape, jnp.float32) * deviation
    if len(shards) > 0:
        result = block_levels(own_key, shape, shards, -0.22, 0.18) * result
    return jnp.clip(result, min=-most, max=most).astype(kind)


def bell_draw_with(rng, dims, scale, most, pieces, heavy, kind=jnp.bfloat16):
    entries = scale * jax.random.normal(rng, dims, jnp.float32)
    if pieces:
        entries = entries * block_levels(rng, dims, pieces, -0.22, 0.18)
    return jnp.clip(with_spikes(entries, jax.random.fold_in(rng, 3), *heavy), -most, most).astype(kind)


def setup_inputs(seed: int = 0) -> dict:
    arg_keys = jax.random.split(jax.random.key(seed), 10)
    return {
        "tokens": noise(arg_keys[0], (LEV, NLAT, NLON, MODEL_WIDTH), 1.0, 6.0, ((1, 4), (2, 64))),
        "cotangent": bell_draw_with(arg_keys[1], (LEV, NLAT, NLON, MODEL_WIDTH), 1.0, 16.0, ((1, 4), (2, 64)), (2, 3, 64, 4.0)),
        "norm_scale_vector": jnp.clip(1.0 + 0.18 * jax.random.normal(arg_keys[2], (MODEL_WIDTH,), jnp.float32), 0.099609375, 1.8984375).astype(jnp.bfloat16),
        "query_matrix": draw_query_matrix(jax.random.fold_in(arg_keys[9], 71), 0),
        "key_matrix": draw_key_matrix(jax.random.fold_in(arg_keys[9], 71), 0),
        "value_matrix": noise(arg_keys[5], (MODEL_WIDTH, MODEL_WIDTH), MODEL_WIDTH ** -0.5, 0.1875),
        "output_matrix": noise(arg_keys[6], (MODEL_WIDTH, MODEL_WIDTH), MODEL_WIDTH ** -0.5, 0.1875),
        "adapter_down_maps": noise(arg_keys[7], (4, MODEL_WIDTH, ADAPTER_RANK), MODEL_WIDTH ** -0.5, 0.1875),
        "adapter_up_maps": noise(arg_keys[8], (4, ADAPTER_RANK, MODEL_WIDTH), ADAPTER_RANK ** -0.5, 1.0),
    }


EPS = 1e-05
NEG = -1e+30

def normalize(values):
    center = values - lax.optimization_barrier(jnp.mean(values, axis=-1, keepdims=True))
    spread = lax.optimization_barrier(jnp.mean(center * center, axis=-1, keepdims=True))
    inverse = lax.rsqrt(spread + EPS)
    return (center * inverse, inverse)

def norm_back(upstream_gradient, norm_scale, centred, inverse):
    scaled = upstream_gradient.astype(jnp.float32) * norm_scale
    first_mean = lax.optimization_barrier(jnp.mean(scaled, axis=-1, keepdims=True))
    second_mean = lax.optimization_barrier(jnp.mean(scaled * centred, axis=-1, keepdims=True))
    return inverse * (scaled - first_mean - centred * second_mean)

def partition(region, span_lev, span_lat, span_lon):
    levels, lat_count, lon_count, features = region.shape
    tiles = region.reshape(levels // span_lev, span_lev, lat_count // span_lat, span_lat, lon_count // span_lon, span_lon, features)
    tiles = tiles.transpose(0, 2, 4, 1, 3, 5, 6)
    return tiles.reshape(-1, span_lev * span_lat * span_lon, features)

def unpartition(windows, layout, span_lev, span_lat, span_lon):
    levels, lat_count, lon_count, features = layout
    tiles = windows.reshape(levels // span_lev, lat_count // span_lat, lon_count // span_lon, span_lev, span_lat, span_lon, features)
    tiles = tiles.transpose(0, 3, 1, 4, 2, 5, 6)
    return tiles.reshape(levels, lat_count, lon_count, features)

def matrix_product(left, right):
    return jnp.dot(left, right, preferred_element_type=jnp.float32)

def forward_rows(normalized_rows, upstream_gradient, weight_list, adapter_down_maps, adapter_up_maps):
    projected_rows = []
    lowrank_states = []
    for projection_member in range(3):
        lowrank_state = matrix_product(normalized_rows, adapter_down_maps[projection_member]).astype(jnp.bfloat16)
        built_result = matrix_product(normalized_rows, weight_list[projection_member]) + matrix_product(lowrank_state, adapter_up_maps[projection_member])
        projected_rows.append(built_result.astype(jnp.bfloat16))
        lowrank_states.append(lowrank_state)
    backward_output = matrix_product(upstream_gradient, adapter_up_maps[3].T).astype(jnp.bfloat16)
    attention_gradient = (matrix_product(upstream_gradient, weight_list[3].T) + matrix_product(backward_output, adapter_down_maps[3].T)).astype(jnp.bfloat16)
    return (projected_rows, attention_gradient, lowrank_states, backward_output)

def attend(queries, key_rows, value_rows, attention_gradient, labels, heads):
    windows, window_extent, features = queries.shape
    head_size = features // heads

    def per_head(tensor):
        return tensor.reshape(windows, window_extent, heads, head_size).astype(jnp.float32)
    query_h = per_head(queries)
    key_h = per_head(key_rows)
    value_h = per_head(value_rows)
    grad_h = per_head(attention_gradient)
    factor = head_size ** (-0.5)
    scores = jnp.einsum('wqhd,wkhd->whqk', query_h, key_h) * factor
    allowed = labels[:, None, :, None] == labels[:, None, None, :]
    scores = jnp.where(allowed, scores, NEG)
    raised = jnp.exp(scores - lax.optimization_barrier(jnp.max(scores, axis=-1, keepdims=True)))
    probs = raised / lax.optimization_barrier(jnp.sum(raised, axis=-1, keepdims=True))
    probs_low = probs.astype(jnp.bfloat16).astype(jnp.float32)
    attended_rows = jnp.einsum('whqk,wkhd->wqhd', probs_low, value_h)
    dprob = jnp.einsum('wqhd,wkhd->whqk', grad_h, value_h)
    dscore = probs * (dprob - lax.optimization_barrier(jnp.sum(dprob * probs, axis=-1, keepdims=True))) * factor
    dscore = dscore.astype(jnp.bfloat16).astype(jnp.float32)
    dquery = jnp.einsum('whqk,wkhd->wqhd', dscore, key_h)
    dkey = jnp.einsum('whqk,wqhd->wkhd', dscore, query_h)
    dvalue = jnp.einsum('whqk,wqhd->wkhd', probs_low, grad_h)

    def merged(tensor):
        return tensor.astype(jnp.bfloat16).reshape(windows, window_extent, features)
    return (merged(attended_rows), merged(dquery), merged(dkey), merged(dvalue))

def backward_rows(normalized_rows, upstream_gradient, attended_rows, gradient_list, lowrank_states, backward_output, weight_list, adapter_down_maps, adapter_up_maps):
    lowrank_output = matrix_product(attended_rows, adapter_down_maps[3]).astype(jnp.bfloat16)
    summed_rows = jnp.zeros(normalized_rows.shape, jnp.float32)
    gradient_couples = []
    for projection_member in range(3):
        gradient_value = gradient_list[projection_member]
        backward_lowrank = matrix_product(gradient_value, adapter_up_maps[projection_member].T).astype(jnp.bfloat16)
        gradient_couples.append((matrix_product(normalized_rows.T, backward_lowrank), matrix_product(lowrank_states[projection_member].T, gradient_value)))
        summed_rows = summed_rows + matrix_product(gradient_value, weight_list[projection_member].T) + matrix_product(backward_lowrank, adapter_down_maps[projection_member].T)
    gradient_couples.append((matrix_product(attended_rows.T, backward_output), matrix_product(lowrank_output.T, upstream_gradient)))
    return (summed_rows.astype(jnp.bfloat16), gradient_couples)

def reference(tokens, cotangent, norm_scale_vector, query_matrix, key_matrix, value_matrix, output_matrix, adapter_down_maps, adapter_up_maps):
    norm_scale = norm_scale_vector.astype(jnp.float32)
    centred, inverse = normalize(tokens.astype(jnp.float32))
    normed = (centred * norm_scale).astype(jnp.bfloat16)
    offsets = (-1, -(WLAT // 2), -(WLON // 2))
    moved = jnp.roll(normed, offsets, (0, 1, 2))
    pushed = jnp.roll(cotangent, offsets, (0, 1, 2))
    level_flag = 2 * (jnp.arange(LEV, dtype=jnp.int32) == LEV - 1).astype(jnp.int32)
    band_flag = (jnp.arange(NLAT, dtype=jnp.int32) >= NLAT - WLAT // 2).astype(jnp.int32)
    label_grid = level_flag[:, None, None, None] + band_flag[None, :, None, None] + jnp.zeros((1, 1, NLON, 1), jnp.int32)
    window_extent = WLEV * WLAT * WLON
    lines = LEV // WLEV * (NLAT // WLAT)
    across_heads = NLON // WLON
    normed_win = partition(moved, WLEV, WLAT, WLON).reshape(lines, across_heads, window_extent, MODEL_WIDTH)
    pushed_win = partition(pushed, WLEV, WLAT, WLON).reshape(lines, across_heads, window_extent, MODEL_WIDTH)
    label_win = partition(label_grid, WLEV, WLAT, WLON).reshape(lines, across_heads, window_extent)
    weight_list = (query_matrix, key_matrix, value_matrix, output_matrix)

    def one_line(packed):
        normed_line, pushed_line, label_line = packed
        normalized_rows = normed_line.reshape(across_heads * window_extent, MODEL_WIDTH)
        upstream_gradient = pushed_line.reshape(across_heads * window_extent, MODEL_WIDTH)
        projected_rows, attention_gradient, lowrank_states, backward_output = forward_rows(normalized_rows, upstream_gradient, weight_list, adapter_down_maps, adapter_up_maps)
        shaped = [tensor.reshape(across_heads, window_extent, MODEL_WIDTH) for tensor in projected_rows + [attention_gradient]]
        attended_rows, dquery, dkey, dvalue = attend(shaped[0], shaped[1], shaped[2], shaped[3], label_line, HEADS)
        gradient_list = [tensor.reshape(across_heads * window_extent, MODEL_WIDTH) for tensor in (dquery, dkey, dvalue)]
        summed_rows, gradient_couples = backward_rows(normalized_rows, upstream_gradient, attended_rows.reshape(across_heads * window_extent, MODEL_WIDTH), gradient_list, lowrank_states, backward_output, weight_list, adapter_down_maps, adapter_up_maps)
        down_part = jnp.concatenate([pair[0] for pair in gradient_couples], 0)
        up_part = jnp.concatenate([pair[1] for pair in gradient_couples], 1)
        return (summed_rows.reshape(across_heads, window_extent, MODEL_WIDTH), down_part, up_part)
    dh_win, down_parts, up_parts = lax.map(one_line, (normed_win, pushed_win, label_win))
    dh_shift = unpartition(dh_win.reshape(-1, window_extent, MODEL_WIDTH), (LEV, NLAT, NLON, MODEL_WIDTH), WLEV, WLAT, WLON)
    dnormed = jnp.roll(dh_shift, (1, WLAT // 2, WLON // 2), (0, 1, 2))
    tokens_grad = (cotangent.astype(jnp.float32) + norm_back(dnormed, norm_scale, centred, inverse)).astype(jnp.bfloat16)
    grad_scale = float(TOKENS) ** (-0.5)
    return (tokens_grad, lax.optimization_barrier(jnp.sum(down_parts, axis=0)) * grad_scale, lax.optimization_barrier(jnp.sum(up_parts, axis=0)) * grad_scale)
```

```python
import functools

import jax
import jax.numpy as jnp
import numpy as np
from jax import lax
from jax.experimental import pallas as pl
from jax.experimental.pallas import tpu as pltpu
from jax.sharding import PartitionSpec as P

MESH = pl.DeviceIdType.MESH
BF = jnp.bfloat16
F32 = jnp.float32
EPS = 1e-05
NEG = -1e30
D = 1024
WIN = 144
TOK = 2 * WIN
LEVELS = ((1, 2), (3, 0))
OWN = (3, 0)
VMEM_LIMIT = 60 * 1024 * 1024


def permutation_table():
    table = np.zeros((592, 128), np.float32)

    def source(h, t):
        return (t // 18) * 48 + (t // 6 % 3) * 16 + 6 * h + t % 6

    for h in range(2):
        for t in range(32):
            table[32 * h + t, source(h, t)] = 1
            table[192 + source(h, t), 32 * h + t] = 1
        for k in range(4):
            for t in range(4):
                table[64 + 32 * k + 16 * h + 4 * k + t, source(h, 32 + t)] = 1
                table[288 + 96 * 0 + source(h, 32 + t), 32 * k + 16 * h + 4 * k + t] = 1
    for p in range(4):
        for k in range(4):
            for t in range(4):
                table[384 + 16 * k + 4 * p + t, 16 * p + 4 * k + t] = 1
                table[448 + 16 * p + 4 * k + t, 16 * k + 4 * p + t] = 1
    return table[:512]


def dot(a, b):
    return jnp.dot(a, b, preferred_element_type=F32)


def dot_nt(a, b):
    return lax.dot_general(a, b, (((1,), (1,)), ((), ())), preferred_element_type=F32)


def dot_tn(a, b):
    return lax.dot_general(a, b, (((0,), (0,)), ((), ())), preferred_element_type=F32)


def neighbour(sizes, lat_step, lon_step):
    lon = lax.rem(lax.axis_index("lon") + lon_step + sizes["lon"], sizes["lon"])
    lat = lax.rem(lax.axis_index("lat") + lat_step + sizes["lat"], sizes["lat"])
    return (lon, lat)


def steps_of(w, p):
    differs = p ^ OWN[w]
    sign = -1 if w == 0 else 1
    return sign * (differs >> 1), sign * (differs & 1)


def moving_pieces():
    return [(w, p) for w in range(2) for p in range(4) if p != OWN[w]]


def ring_of(sizes):
    return [neighbour(sizes, *steps_of(w, p)) for w, p in moving_pieces()]


def stage_slabs(array_ref, stage):
    stage[...] = jnp.zeros_like(stage)
    for w in range(2):
        for lv in range(2):
            for a in range(6):
                row = lv * 48 + (a % 3) * 16
                stage[w, a // 3, row : row + 12, :] = array_ref[LEVELS[w][lv], a]


def pack(stage, table, main, tail):
    for w in range(2):
        for ah in range(2):
            rows = stage[w, ah]
            packed = dot(table[0:64, 0:96], rows).astype(BF)
            main[w, 2 * ah] = packed[0:32]
            main[w, 2 * ah + 1] = packed[32:64]
            ends = jnp.zeros((32, 256), F32)
            for k in range(4):
                ends = ends + dot(
                    table[64 + 32 * k : 96 + 32 * k, 0:96], rows[:, 256 * k : 256 * k + 256]
                )
            ends = ends.astype(BF)
            tail[w, 2 * ah] = ends[0:16]
            tail[w, 2 * ah + 1] = ends[16:32]


def tails_to_window(table, tails, window, first):
    stacked = tails.reshape(64, 256)
    for k in range(4):
        window[first + 128 : first + 144, 256 * k : 256 * k + 256] = dot(
            table[384 + 16 * k : 400 + 16 * k, 0:64], stacked
        ).astype(BF)


def window_to_tails(table, rows):
    ends = jnp.zeros((64, 256), F32)
    for k in range(4):
        ends = ends + dot(
            table[448:512, 16 * k : 16 * k + 16], rows[:, 256 * k : 256 * k + 256]
        )
    return ends.astype(BF).reshape(4, 16, 256)


def unpack(table, main, tail, out_ref):
    for w in range(2):
        for ah in range(2):
            ends = jnp.concatenate([tail[w, 2 * ah], tail[w, 2 * ah + 1]], 0)
            rows = jnp.concatenate([main[w, 2 * ah], main[w, 2 * ah + 1]], 0)
            for k in range(4):
                cols = slice(256 * k, 256 * k + 256)
                slabs = (
                    dot(table[192:288, 0:64], rows[:, cols])
                    + dot(table[288:384, 32 * k : 32 * k + 32], ends)
                ).astype(BF)
                for lv in range(2):
                    for a in range(3):
                        row = lv * 48 + a * 16
                        out_ref[LEVELS[w][lv], 3 * ah + a, :, cols] = slabs[row : row + 12]


def barrier_with(devices):
    barrier = pltpu.get_barrier_semaphore()
    for device in devices:
        pl.semaphore_signal(barrier, inc=1, device_id=device, device_id_type=MESH)
    pl.semaphore_wait(barrier, len(devices))


def remote(src, dst, send, recv, device):
    return pltpu.make_async_remote_copy(
        src_ref=src, dst_ref=dst, send_sem=send, recv_sem=recv, device_id=device, device_id_type=MESH
    )


def in_copies(sizes, which, main, tail, window, tails, send, recv):
    copies = []
    for w, p in moving_pieces():
        device = neighbour(sizes, *steps_of(w, p))
        copies.append(
            remote(
                main.at[w, p],
                window.at[pl.ds(WIN * w + 32 * p, 32)],
                send.at[which, w, p, 0],
                recv.at[which, w, p, 0],
                device,
            )
        )
        copies.append(
            remote(
                tail.at[w, p],
                tails.at[w, p],
                send.at[which, w, p, 1],
                recv.at[which, w, p, 1],
                device,
            )
        )
    return copies


def keep_own(main, tail, window, tails):
    for w in range(2):
        p = OWN[w]
        window[WIN * w + 32 * p : WIN * w + 32 * p + 32, :] = main[w, p]
        tails[w, p] = tail[w, p]


def exchange_in(sizes, tok, cot, table, w_tok, w_cot, stage, main, tail, tails, send, recv):
    barrier_with(ring_of(sizes))
    copies = []
    for which, (array, window) in enumerate(((tok, w_tok), (cot, w_cot))):
        stage_slabs(array, stage)
        pack(stage, table, main.at[which], tail.at[which])
        own = in_copies(
            sizes, which, main.at[which], tail.at[which], window, tails.at[which], send, recv
        )
        for copy in own:
            copy.start()
        copies.append(own)
        keep_own(main.at[which], tail.at[which], window, tails.at[which])
    for which, window in enumerate((w_tok, w_cot)):
        for copy in copies[which]:
            copy.wait()
        for w in range(2):
            tails_to_window(table, tails[which, w], window, WIN * w)


def slot_lanes(values, slots):
    lane = lax.broadcasted_iota(jnp.int32, values.shape, 1) // 32
    keep = lane == slots[0]
    for slot in slots[1:]:
        keep = keep | (lane == slot)
    return jnp.where(keep, values, 0.0)


def norm_rows(w_tok, scale, hs, mean, rstd):
    gain = scale[...].astype(F32)

    def body(i, carry):
        rows = pl.ds(pl.multiple_of(i * 32, 32), 32)
        x = w_tok[rows, :].astype(F32)
        mu = jnp.mean(x, axis=-1, keepdims=True)
        center = x - mu
        inverse = lax.rsqrt(jnp.mean(center * center, axis=-1, keepdims=True) + EPS)
        mean[rows, :] = mu
        rstd[rows, :] = inverse
        hs[rows, :] = (center * inverse * gain).astype(BF)
        return carry

    lax.fori_loop(0, TOK // 32, body, 0)


def adapter_tables(down, acat):
    acat[...] = jnp.concatenate([down[n] for n in range(4)], 1)


def project(hs, w_cot, weights, up, acat, low, back, q, k, v, da):
    ups = up[...].reshape(128, D)
    low[...] = dot(hs[...], acat[...]).astype(BF)
    back[...] = slot_lanes(dot_nt(w_cot[...], ups), (3,)).astype(BF)
    lows = [slot_lanes(low[...].astype(F32), (n,)).astype(BF) for n in range(3)]
    wq, wk, wv, wo = weights
    for c in range(4):
        cols = slice(256 * c, 256 * c + 256)
        for n, (w, out) in enumerate(((wq, q), (wk, k), (wv, v))):
            out[:, cols] = (dot(hs[...], w[:, cols]) + dot(lows[n], ups[:, cols])).astype(BF)
        da[:, cols] = (dot_nt(w_cot[...], wo[cols, :]) + dot_nt(back[...], acat[cols, :])).astype(BF)


def make_bias(sizes, bias):
    lat = lax.axis_index("lat")

    def coordinates(r):
        tail = r >= 128
        piece = jnp.where(tail, (r - 128) // 4, r // 32)
        t = jnp.where(tail, 32 + r % 4, r % 32)
        return (piece < 2).astype(jnp.int32), (t >= 18).astype(jnp.int32)

    key_ah, key_lv = coordinates(lax.broadcasted_iota(jnp.int32, (WIN, 4 * WIN), 0))
    c = lax.broadcasted_iota(jnp.int32, (WIN, 4 * WIN), 1)
    for n in (3, 2, 1):
        c = jnp.where(c >= n * WIN, c - n * WIN, c)
    query_ah, query_lv = coordinates(c)
    for w in range(2):
        last = (lat == (sizes["lat"] - 1 if w == 0 else 0)).astype(jnp.int32)
        differs = (key_ah != query_ah).astype(jnp.int32) * last
        if w == 1:
            differs = differs + (key_lv != query_lv).astype(jnp.int32)
        bias[w] = jnp.where(differs > 0, NEG, 0.0).astype(F32)


def attend(q, k, v, da, bias, at, dq, dk, dv):
    lane = lax.broadcasted_iota(jnp.int32, (1, 256), 1) // 64
    masks = [(lane == h).astype(F32).astype(BF) for h in range(4)]
    lanes = lax.broadcasted_iota(jnp.int32, (WIN, 256), 1) // 64

    def stacked(values):
        return jnp.concatenate([values * mask for mask in masks], 0)

    def own_blocks(values):
        result = values[0:WIN]
        for h in range(1, 4):
            result = jnp.where(lanes == h, values[WIN * h : WIN * h + WIN], result)
        return result

    def body(c, carry):
        cols = pl.ds(pl.multiple_of(c * 256, 256), 256)
        for w in range(2):
            rows = pl.ds(WIN * w, WIN)
            kk = k[rows, cols]
            vv = v[rows, cols]
            q4 = stacked(q[rows, cols] * jnp.asarray(0.125, BF))
            d4 = stacked(da[rows, cols])
            s = dot_nt(kk, q4) + bias[w]
            e = jnp.exp(s - jnp.max(s, axis=0, keepdims=True))
            p = e * (1.0 / jnp.sum(e, axis=0, keepdims=True))
            dp = dot_nt(vv, d4)
            ds = (p * (dp - jnp.sum(dp * p, axis=0, keepdims=True))).astype(BF)
            pb = p.astype(BF)
            dv[rows, cols] = dot(pb, d4).astype(BF)
            dk[rows, cols] = dot(ds, q4).astype(BF)
            at[rows, cols] = own_blocks(dot_tn(pb, vv)).astype(BF)
            dq[rows, cols] = (own_blocks(dot_tn(ds, kk)) * 0.125).astype(BF)
        return carry

    lax.fori_loop(0, 4, body, 0)


def lora_partials(hs, w_cot, at, dq, dk, dv, up, acat, low, back, gt):
    ups = up[...].reshape(128, D)
    lane = lax.broadcasted_iota(jnp.int32, (TOK, 128), 1) // 32
    backs = back[...].astype(F32)
    for n, d in enumerate((dq, dk, dv)):
        backs = jnp.where(lane == n, dot_nt(d[...], ups), backs)
    back[...] = backs.astype(BF)
    lows = jnp.where(lane == 3, dot(at[...], acat[...]), low[...].astype(F32))
    back_t = backs.T.astype(BF)
    low_t = lows.T.astype(BF)
    for c in range(4):
        cols = slice(256 * c, 256 * c + 256)
        own_down = dot(back_t[0:96], hs[:, cols])
        last_down = dot(back_t[96:128], at[:, cols])
        ups_own = [dot(low_t[32 * n : 32 * n + 32], d[:, cols]) for n, d in enumerate((dq, dk, dv, w_cot))]
        parts = []
        for n in range(4):
            parts.append(own_down[32 * n : 32 * n + 32] if n < 3 else last_down)
            parts.append(ups_own[n])
        block = jnp.concatenate(parts, 0)
        for half in range(2):
            turned = block[:, 128 * half : 128 * half + 128].T.astype(BF)
            for b in range(8):
                f = 16 * c + 8 * half + b
                gt[f % 2, f // 2 % 2, f // 4 % 4, f // 16] = turned[16 * b : 16 * b + 16]


def input_gradient(w_tok, w_cot, scale, weights, dq, dk, dv, acat, back, mean, rstd, dh, tg):
    gain = scale[...].astype(F32)
    backs = slot_lanes(back[...].astype(F32), (0, 1, 2)).astype(BF)
    for c in range(4):
        cols = slice(256 * c, 256 * c + 256)
        total = dot_nt(backs, acat[cols, :])
        for w, d in zip(weights[:3], (dq, dk, dv)):
            total = total + dot_nt(d[...], w[cols, :])
        dh[:, cols] = total.astype(BF)

    def body(i, carry):
        rows = pl.ds(pl.multiple_of(i * 32, 32), 32)
        inverse = rstd[rows, :]
        xhat = (w_tok[rows, :].astype(F32) - mean[rows, :]) * inverse
        g = dh[rows, :].astype(F32) * gain
        first = jnp.mean(g, axis=-1, keepdims=True)
        second = jnp.mean(g * xhat, axis=-1, keepdims=True)
        tg[rows, :] = (w_cot[rows, :].astype(F32) + inverse * (g - first - xhat * second)).astype(BF)
        return carry

    lax.fori_loop(0, TOK // 32, body, 0)


def compute(
    sizes, w_tok, w_cot, scale, wq, wk, wv, wo, down, up, table, tg, tg_tail, gt,
    hs, q, k, v, da, at, dq, dk, dv, acat, low, back, mean, rstd, bias, dh,
):
    weights = (wq, wk, wv, wo)
    make_bias(sizes, bias)
    adapter_tables(down, acat)
    norm_rows(w_tok, scale, hs, mean, rstd)
    project(hs, w_cot, weights, up, acat, low, back, q, k, v, da)
    attend(q, k, v, da, bias, at, dq, dk, dv)
    lora_partials(hs, w_cot, at, dq, dk, dv, up, acat, low, back, gt)
    input_gradient(w_tok, w_cot, scale, weights, dq, dk, dv, acat, back, mean, rstd, dh, tg)
    for w in range(2):
        tg_tail[w] = window_to_tails(table, tg[WIN * w + 128 : WIN * w + 144, :])


def out_copies(sizes, tg, tg_tail, main, tail, send, recv):
    copies = []
    for w, p in moving_pieces():
        lat_step, lon_step = steps_of(w, p)
        device = neighbour(sizes, -lat_step, -lon_step)
        copies.append(
            remote(
                tg.at[pl.ds(WIN * w + 32 * p, 32)], main.at[w, p],
                send.at[w, p, 0], recv.at[w, p, 0], device,
            )
        )
        copies.append(
            remote(
                tg_tail.at[w, p], tail.at[w, p], send.at[w, p, 1], recv.at[w, p, 1], device
            )
        )
    return copies


class Reducer:
    def __init__(self):
        lon = lax.axis_index("lon")
        lat = lax.axis_index("lat")
        self.y = lax.rem(lon, 4)
        self.zx = lon // 4
        self.core = lax.rem(lat, 2)
        self.xl = lat // 2
        self.first = (lon, self.xl * 2 + 1 - self.core)
        self.second = []
        for n in range(1, 8):
            y = lax.rem(self.y + n // 2, 4)
            xl = lax.rem(self.xl + n % 2, 2)
            self.second.append((n - 1, y, xl, (self.zx * 4 + y, xl * 2 + self.core)))
        self.third = []
        for n in range(1, 16):
            zx = lax.rem(self.zx + n, 16)
            self.third.append((n - 1, zx, (zx * 4 + self.y, lat)))

    def partners(self):
        return [self.first] + [s[-1] for s in self.second] + [s[-1] for s in self.third]

    def start_first(self, gt, r1, sems):
        copy = remote(gt.at[1 - self.core], r1, sems.at[0, 0], sems.at[1, 0], self.first)
        copy.start()
        return copy

    def start_second(self, copy, gt, r1, s1, r2, sems):
        copy.wait()
        s1[...] = (gt[self.core].astype(F32) + r1[...].astype(F32)).astype(BF)
        copies = []
        for n, y, xl, device in self.second:
            copies.append(remote(s1.at[xl, y], r2.at[n], sems.at[0, 1 + n], sems.at[1, 1 + n], device))
            copies[-1].start()
        return copies

    def start_third(self, copies, s1, r2, s2, r3, sems):
        total = s1[self.xl, self.y].astype(F32)
        for copy in copies:
            copy.wait()
        for n in range(7):
            total = total + r2[n].astype(F32)
        for half in range(2):
            s2[half] = total[:, :, 128 * half : 128 * half + 128].astype(BF)
        copies = []
        for n, zx, device in self.third:
            copies.append(
                remote(
                    s2.at[zx // 8, lax.rem(zx, 4)], r3.at[n], sems.at[0, 8 + n], sems.at[1, 8 + n], device
                )
            )
            copies[-1].start()
        return copies

    def finish(self, copies, s2, r3, down_out, up_out, factor):
        total = s2[self.zx // 8, lax.rem(self.zx, 4)].astype(F32)
        for copy in copies:
            copy.wait()
        for n in range(15):
            total = total + r3[n].astype(F32)
        total = total * factor
        own = jnp.where(lax.rem(self.zx // 4, 2) == 0, total[:, 0:64], total[:, 64:128])
        down_out[...] = own[:, 0:32]
        up_out[...] = own[:, 32:64].T


REDUCE_SCRATCH = [
    pltpu.VMEM((2, 4, 4, 16, 256), BF),
    pltpu.VMEM((2, 4, 4, 16, 256), BF),
    pltpu.VMEM((7, 4, 16, 256), BF),
    pltpu.VMEM((2, 4, 16, 128), BF),
    pltpu.VMEM((15, 16, 128), BF),
    pltpu.SemaphoreType.DMA((2, 23)),
]


def finish_kernel(
    sizes, factor, tg, tg_tail, gt, table, grad_out, down_out, up_out,
    main, tail, send, recv, r1, s1, r2, s2, r3, sems,
):
    reducer = Reducer()
    barrier_with(ring_of(sizes) + reducer.partners())
    first = reducer.start_first(gt, r1, sems)
    copies = out_copies(sizes, tg, tg_tail, main, tail, send, recv)
    for copy in copies:
        copy.start()
    second = reducer.start_second(first, gt, r1, s1, r2, sems)
    for w in range(2):
        p = OWN[w]
        main[w, p] = tg[WIN * w + 32 * p : WIN * w + 32 * p + 32, :]
        tail[w, p] = tg_tail[w, p]
    third = reducer.start_third(second, s1, r2, s2, r3, sems)
    for copy in copies:
        copy.wait()
    unpack(table, main, tail, grad_out)
    reducer.finish(third, s2, r3, down_out, up_out, factor)


def vmem(n):
    return [pl.BlockSpec(memory_space=pltpu.VMEM)] * n


def local(
    sizes, tokens, cotangent, norm_scale_vector, query_matrix, key_matrix, value_matrix, output_matrix,
    adapter_down_maps, adapter_up_maps,
):
    table = jnp.asarray(permutation_table(), BF)
    factor = float(TOK * sizes["lon"] * sizes["lat"]) ** (-0.5)
    rows = jax.ShapeDtypeStruct((TOK, D), BF)
    w_tok, w_cot = pl.pallas_call(
        functools.partial(exchange_in, sizes),
        out_shape=(rows, rows),
        in_specs=vmem(3),
        out_specs=tuple(vmem(2)),
        scratch_shapes=[
            pltpu.VMEM((2, 2, 96, D), BF),
            pltpu.VMEM((2, 2, 4, 32, D), BF),
            pltpu.VMEM((2, 2, 4, 16, 256), BF),
            pltpu.VMEM((2, 2, 4, 16, 256), BF),
            pltpu.SemaphoreType.DMA((2, 2, 4, 2)),
            pltpu.SemaphoreType.DMA((2, 2, 4, 2)),
        ],
        compiler_params=pltpu.CompilerParams(
            collective_id=0, has_side_effects=True, vmem_limit_bytes=VMEM_LIMIT
        ),
    )(tokens, cotangent, table)
    tg, tg_tail, gt = pl.pallas_call(
        functools.partial(compute, sizes),
        out_shape=(
            rows,
            jax.ShapeDtypeStruct((2, 4, 16, 256), BF),
            jax.ShapeDtypeStruct((2, 2, 4, 4, 16, 256), BF),
        ),
        in_specs=vmem(10),
        out_specs=tuple(vmem(3)),
        scratch_shapes=[pltpu.VMEM((TOK, D), BF)] * 9
        + [
            pltpu.VMEM((D, 128), BF),
            pltpu.VMEM((TOK, 128), BF),
            pltpu.VMEM((TOK, 128), BF),
            pltpu.VMEM((TOK, 1), F32),
            pltpu.VMEM((TOK, 1), F32),
            pltpu.VMEM((2, WIN, 4 * WIN), F32),
            pltpu.VMEM((TOK, D), BF),
        ],
        compiler_params=pltpu.CompilerParams(vmem_limit_bytes=VMEM_LIMIT),
    )(
        w_tok, w_cot, norm_scale_vector.reshape(1, D), query_matrix, key_matrix, value_matrix, output_matrix,
        adapter_down_maps, adapter_up_maps, table,
    )
    return pl.pallas_call(
        functools.partial(finish_kernel, sizes, factor),
        out_shape=(
            jax.ShapeDtypeStruct(tokens.shape, BF),
            jax.ShapeDtypeStruct((16, 32), F32),
            jax.ShapeDtypeStruct((32, 16), F32),
        ),
        in_specs=vmem(4),
        out_specs=tuple(vmem(3)),
        scratch_shapes=[
            pltpu.VMEM((2, 4, 32, D), BF),
            pltpu.VMEM((2, 4, 16, 256), BF),
            pltpu.SemaphoreType.DMA((2, 4, 2)),
            pltpu.SemaphoreType.DMA((2, 4, 2)),
        ]
        + REDUCE_SCRATCH,
        compiler_params=pltpu.CompilerParams(
            collective_id=1, has_side_effects=True, vmem_limit_bytes=VMEM_LIMIT
        ),
    )(tg, tg_tail, gt, table)


def solution(mesh):
    sizes = dict(mesh.shape)
    spread = P(None, "lat", "lon", None)
    return jax.shard_map(
        functools.partial(local, sizes),
        mesh=mesh,
        in_specs=(spread, spread, P(), P(), P(), P(), P(), P(), P()),
        out_specs=(spread, P(("lon", "lat"), None), P(None, ("lon", "lat"))),
        check_vma=False,
    )
```

```python
import functools

import jax
import jax.numpy as jnp
import numpy as np
from jax import lax
from jax.experimental import pallas as pl
from jax.experimental.pallas import tpu as pltpu
from jax.sharding import PartitionSpec as P

MESH = pl.DeviceIdType.MESH
BF = jnp.bfloat16
F32 = jnp.float32
EPS = 1e-05
NEG = -1e30
D = 1024
WIN = 144
TOK = 2 * WIN
LEVELS = ((1, 2), (3, 0))
OWN = (3, 0)
VMEM_LIMIT = 60 * 1024 * 1024


def move_tables():
    pack = np.zeros((384, 144), np.float32)
    unpack = np.zeros((288, 256), np.float32)
    ends = np.zeros((128, 64), np.float32)

    def source(w, h, t):
        return (t // 6 % 3) * 48 + (6 * h + t % 6) * 4 + LEVELS[w][t // 18]

    for w in range(2):
        for h in range(2):
            for t in range(32):
                row = 64 * w + 32 * h + t
                pack[row, source(w, h, t)] = 1
                unpack[source(w, h, t), row] = 1
            for k in range(4):
                for t in range(4):
                    row = 32 * w + 16 * h + 4 * k + t
                    pack[128 + 64 * k + row, source(w, h, 32 + t)] = 1
                    unpack[144 + source(w, h, 32 + t), 64 * k + row] = 1
    for p in range(4):
        for k in range(4):
            for t in range(4):
                ends[16 * k + 4 * p + t, 16 * p + 4 * k + t] = 1
                ends[64 + 16 * p + 4 * k + t, 16 * k + 4 * p + t] = 1
    return tuple(jnp.asarray(table, BF) for table in (pack, unpack, ends))


def dot(a, b):
    return jnp.dot(a, b, preferred_element_type=F32)


def dot_nt(a, b):
    return lax.dot_general(a, b, (((1,), (1,)), ((), ())), preferred_element_type=F32)


def dot_tn(a, b):
    return lax.dot_general(a, b, (((0,), (0,)), ((), ())), preferred_element_type=F32)


def neighbour(sizes, lat_step, lon_step):
    lon = lax.rem(lax.axis_index("lon") + lon_step + sizes["lon"], sizes["lon"])
    lat = lax.rem(lax.axis_index("lat") + lat_step + sizes["lat"], sizes["lat"])
    return (lon, lat)


def steps_of(w, p):
    differs = p ^ OWN[w]
    sign = -1 if w == 0 else 1
    return sign * (differs >> 1), sign * (differs & 1)


def moving_pieces():
    return [(w, p) for w in range(2) for p in range(4) if p != OWN[w]]


def ring_of(sizes):
    return [neighbour(sizes, *steps_of(w, p)) for w, p in moving_pieces()]


def remote(src, dst, send, recv, device):
    return pltpu.make_async_remote_copy(
        src_ref=src, dst_ref=dst, send_sem=send, recv_sem=recv, device_id=device, device_id_type=MESH
    )


def natural_rows(raw, wide):
    for a in range(6):
        for o in range(12):
            row = (12 * a + o) * 4
            wide[row : row + 4, :] = raw[a, o].astype(F32)


def piece_rows(w, p):
    return p >> 1, 64 * w + 32 * (p & 1)


def pack(wide, table, main, tail):
    for ah in range(2):
        rows = wide[WIN * ah : WIN * ah + WIN, :].astype(BF)
        main[ah] = dot(table[0:128, :], rows).astype(BF)
        ends = dot(table[128:192, :], rows[:, 0:256])
        for k in range(1, 4):
            ends = ends + dot(
                table[128 + 64 * k : 192 + 64 * k, :], rows[:, 256 * k : 256 * k + 256]
            )
        tail[ah] = ends.astype(BF)


def tails_to_window(table, tails, window, first):
    stacked = tails.reshape(64, 256)
    for k in range(4):
        window[first + 128 : first + 144, 256 * k : 256 * k + 256] = dot(
            table[16 * k : 16 * k + 16, :], stacked
        ).astype(BF)


def window_to_tails(table, rows):
    ends = jnp.zeros((64, 256), F32)
    for k in range(4):
        ends = ends + dot(
            table[64:128, 16 * k : 16 * k + 16], rows[:, 256 * k : 256 * k + 256]
        )
    return ends.astype(BF).reshape(4, 16, 256)


def in_copies(sizes, main, tail, window, tails, send, recv):
    copies = []
    for w, p in moving_pieces():
        device = neighbour(sizes, *steps_of(w, p))
        ah, row = piece_rows(w, p)
        copies.append(
            remote(
                main.at[ah, pl.ds(row, 32)], window.at[pl.ds(WIN * w + 32 * p, 32)],
                send.at[w, p, 0], recv.at[w, p, 0], device,
            )
        )
        copies.append(
            remote(
                tail.at[ah, pl.ds(row // 2, 16)], tails.at[w, p],
                send.at[w, p, 1], recv.at[w, p, 1], device,
            )
        )
    return copies


def keep_own(main, tail, window, tails):
    for w in range(2):
        p = OWN[w]
        ah, row = piece_rows(w, p)
        window[WIN * w + 32 * p : WIN * w + 32 * p + 32, :] = main[ah, row : row + 32]
        tails[w, p] = tail[ah, row // 2 : row // 2 + 16]


def out_copies(sizes, tg, tg_tail, main, tail, send, recv):
    copies = []
    for w, p in moving_pieces():
        lat_step, lon_step = steps_of(w, p)
        device = neighbour(sizes, -lat_step, -lon_step)
        ah, row = piece_rows(w, p)
        copies.append(
            remote(
                tg.at[pl.ds(WIN * w + 32 * p, 32)], main.at[ah, pl.ds(row, 32)],
                send.at[w, p, 0], recv.at[w, p, 0], device,
            )
        )
        copies.append(
            remote(
                tg_tail.at[w, p], tail.at[ah, pl.ds(row // 2, 16)],
                send.at[w, p, 1], recv.at[w, p, 1], device,
            )
        )
    return copies


def return_own(tg, tg_tail, main, tail):
    for w in range(2):
        p = OWN[w]
        ah, row = piece_rows(w, p)
        main[ah, row : row + 32] = tg[WIN * w + 32 * p : WIN * w + 32 * p + 32, :]
        tail[ah, row // 2 : row // 2 + 16] = tg_tail[w, p]


def start_barrier(devices):
    barrier = pltpu.get_barrier_semaphore()
    for device in devices:
        pl.semaphore_signal(barrier, inc=1, device_id=device, device_id_type=MESH)


def end_barrier(devices):
    pl.semaphore_wait(pltpu.get_barrier_semaphore(), len(devices))


def gain_of(scale):
    rows = scale[...].astype(F32)
    return jnp.concatenate([rows[n : n + 1] for n in range(8)], 1)


def slot_lanes(values, slots):
    lane = lax.broadcasted_iota(jnp.int32, values.shape, 1) // 32
    keep = lane == slots[0]
    for slot in slots[1:]:
        keep = keep | (lane == slot)
    return jnp.where(keep, values, 0.0)


def norm_rows(w_tok, scale, hs, mean, rstd):
    gain = gain_of(scale)

    def body(i, carry):
        rows = pl.ds(pl.multiple_of(i * 32, 32), 32)
        x = w_tok[rows, :].astype(F32)
        mu = jnp.mean(x, axis=-1, keepdims=True)
        center = x - mu
        inverse = lax.rsqrt(jnp.mean(center * center, axis=-1, keepdims=True) + EPS)
        mean[rows, :] = mu
        rstd[rows, :] = inverse
        hs[rows, :] = (center * inverse * gain).astype(BF)
        return carry

    lax.fori_loop(0, TOK // 32, body, 0)


def project_tokens(hs, weights, ups, acat, low, q, k, v):
    low[...] = dot_nt(hs[...], acat[...]).astype(BF)
    lows = [slot_lanes(low[...].astype(F32), (n,)).astype(BF) for n in range(3)]
    for c in range(4):
        cols = slice(256 * c, 256 * c + 256)
        for n, (w, out) in enumerate(zip(weights[:3], (q, k, v))):
            out[:, cols] = (dot(hs[...], w[:, cols]) + dot(lows[n], ups[:, cols])).astype(BF)


def project_cotangent(w_cot, wo, ups, acat, back, da):
    back[...] = slot_lanes(dot_nt(w_cot[...], ups[...]), (3,)).astype(BF)
    for c in range(4):
        cols = slice(256 * c, 256 * c + 256)
        da[:, cols] = (dot_nt(w_cot[...], wo[cols, :]) + dot(back[...], acat[:, cols])).astype(BF)


def make_bias(sizes, bias):
    lat = lax.axis_index("lat")

    def coordinates(r):
        tail = r >= 128
        piece = jnp.where(tail, (r - 128) // 4, r // 32)
        t = jnp.where(tail, 32 + r % 4, r % 32)
        return (piece < 2).astype(jnp.int32), (t >= 18).astype(jnp.int32)

    key_ah, key_lv = coordinates(lax.broadcasted_iota(jnp.int32, (WIN, 4 * WIN), 0))
    c = lax.broadcasted_iota(jnp.int32, (WIN, 4 * WIN), 1)
    for n in (3, 2, 1):
        c = jnp.where(c >= n * WIN, c - n * WIN, c)
    query_ah, query_lv = coordinates(c)
    for w in range(2):
        last = (lat == (sizes["lat"] - 1 if w == 0 else 0)).astype(jnp.int32)
        differs = (key_ah != query_ah).astype(jnp.int32) * last
        if w == 1:
            differs = differs + (key_lv != query_lv).astype(jnp.int32)
        bias[w] = jnp.where(differs > 0, NEG, 0.0).astype(F32)


def attend(q, k, v, da, bias, at, dq, dk, dv):
    lane = lax.broadcasted_iota(jnp.int32, (1, 256), 1) // 64
    masks = [(lane == h).astype(F32).astype(BF) for h in range(4)]
    lanes = lax.broadcasted_iota(jnp.int32, (WIN, 256), 1) // 64

    def stacked(values):
        return jnp.concatenate([values * mask for mask in masks], 0)

    def own_blocks(values):
        result = values[0:WIN]
        for h in range(1, 4):
            result = jnp.where(lanes == h, values[WIN * h : WIN * h + WIN], result)
        return result

    def body(c, carry):
        cols = pl.ds(pl.multiple_of(c * 256, 256), 256)
        for w in range(2):
            rows = pl.ds(WIN * w, WIN)
            kk = k[rows, cols]
            vv = v[rows, cols]
            q4 = stacked(q[rows, cols] * jnp.asarray(0.125, BF))
            d4 = stacked(da[rows, cols])
            s = dot_nt(kk, q4) + bias[w]
            e = jnp.exp(s - jnp.max(s, axis=0, keepdims=True))
            p = e * (1.0 / jnp.sum(e, axis=0, keepdims=True))
            dp = dot_nt(vv, d4)
            ds = (p * (dp - jnp.sum(dp * p, axis=0, keepdims=True))).astype(BF)
            pb = p.astype(BF)
            dv[rows, cols] = dot(pb, d4).astype(BF)
            dk[rows, cols] = dot(ds, q4).astype(BF)
            at[rows, cols] = own_blocks(dot_tn(pb, vv)).astype(BF)
            dq[rows, cols] = (own_blocks(dot_tn(ds, kk)) * 0.125).astype(BF)
        return carry

    lax.fori_loop(0, 4, body, 0)


def lora_partials(hs, w_cot, at, dq, dk, dv, ups, acat, low, back, gt):
    lane = lax.broadcasted_iota(jnp.int32, (TOK, 128), 1) // 32
    backs = back[...].astype(F32)
    for n, d in enumerate((dq, dk, dv)):
        backs = jnp.where(lane == n, dot_nt(d[...], ups[...]), backs)
    back[...] = backs.astype(BF)
    lows = jnp.where(lane == 3, dot_nt(at[...], acat[...]), low[...].astype(F32))
    back_t = backs.T.astype(BF)
    low_t = lows.T.astype(BF)
    for c in range(4):
        cols = slice(256 * c, 256 * c + 256)
        own_down = dot(back_t[0:96], hs[:, cols])
        last_down = dot(back_t[96:128], at[:, cols])
        ups_own = [dot(low_t[32 * n : 32 * n + 32], d[:, cols]) for n, d in enumerate((dq, dk, dv, w_cot))]
        parts = []
        for n in range(4):
            parts.append(own_down[32 * n : 32 * n + 32] if n < 3 else last_down)
            parts.append(ups_own[n])
        block = jnp.concatenate(parts, 0)
        for half in range(2):
            turned = block[:, 128 * half : 128 * half + 128].T.astype(BF)
            for b in range(8):
                f = 16 * c + 8 * half + b
                gt[f % 2, f // 2 % 2, f // 4 % 4, f // 16] = turned[16 * b : 16 * b + 16]


def hidden_gradient(chunks, weights, dq, dk, dv, acat, back, dh):
    backs = slot_lanes(back[...].astype(F32), (0, 1, 2)).astype(BF)
    for c in chunks:
        cols = slice(256 * c, 256 * c + 256)
        total = dot(backs, acat[:, cols])
        for w, d in zip(weights[:3], (dq, dk, dv)):
            total = total + dot_nt(d[...], w[cols, :])
        dh[:, cols] = total.astype(BF)


def norm_gradient(w_tok, w_cot, scale, mean, rstd, dh, tg):
    gain = gain_of(scale)

    def body(i, carry):
        rows = pl.ds(pl.multiple_of(i * 32, 32), 32)
        inverse = rstd[rows, :]
        xhat = (w_tok[rows, :].astype(F32) - mean[rows, :]) * inverse
        g = dh[rows, :].astype(F32) * gain
        first = jnp.mean(g, axis=-1, keepdims=True)
        second = jnp.mean(g * xhat, axis=-1, keepdims=True)
        tg[rows, :] = (w_cot[rows, :].astype(F32) + inverse * (g - first - xhat * second)).astype(BF)
        return carry

    lax.fori_loop(0, TOK // 32, body, 0)


class Reducer:
    def __init__(self):
        lon = lax.axis_index("lon")
        lat = lax.axis_index("lat")
        self.y = lax.rem(lon, 4)
        self.zx = lon // 4
        self.core = lax.rem(lat, 2)
        self.xl = lat // 2
        self.first = (lon, self.xl * 2 + 1 - self.core)
        self.second = []
        for n in range(1, 8):
            y = lax.rem(self.y + n // 2, 4)
            xl = lax.rem(self.xl + n % 2, 2)
            self.second.append((n - 1, y, xl, (self.zx * 4 + y, xl * 2 + self.core)))
        self.third = []
        for n in range(1, 16):
            zx = lax.rem(self.zx + n, 16)
            self.third.append((n - 1, zx, (zx * 4 + self.y, lat)))

    def partners(self):
        return [self.first] + [s[-1] for s in self.second] + [s[-1] for s in self.third]

    def start_first(self, gt, r1, sems):
        copy = remote(gt.at[1 - self.core], r1, sems.at[0, 0], sems.at[1, 0], self.first)
        copy.start()
        return copy

    def start_second(self, copy, gt, r1, s1, r2, sems):
        copy.wait()
        s1[...] = (gt[self.core].astype(F32) + r1[...].astype(F32)).astype(BF)
        copies = []
        for n, y, xl, device in self.second:
            copies.append(remote(s1.at[xl, y], r2.at[n], sems.at[0, 1 + n], sems.at[1, 1 + n], device))
            copies[-1].start()
        return copies

    def start_third(self, copies, s1, r2, s2, r3, sems):
        total = s1[self.xl, self.y].astype(F32)
        for copy in copies:
            copy.wait()
        for n in range(7):
            total = total + r2[n].astype(F32)
        for half in range(2):
            s2[half] = total[:, :, 128 * half : 128 * half + 128].astype(BF)
        copies = []
        for n, zx, device in self.third:
            copies.append(
                remote(
                    s2.at[zx // 8, lax.rem(zx, 4)], r3.at[n], sems.at[0, 8 + n], sems.at[1, 8 + n], device
                )
            )
            copies[-1].start()
        return copies

    def finish(self, copies, s2, r3, out, factor):
        total = s2[self.zx // 8, lax.rem(self.zx, 4)].astype(F32)
        for copy in copies:
            copy.wait()
        for n in range(15):
            total = total + r3[n].astype(F32)
        total = total * factor
        out[...] = jnp.where(lax.rem(self.zx // 4, 2) == 0, total[:, 0:64], total[:, 64:128])


REDUCE_SCRATCH = [
    pltpu.VMEM((2, 2, 4, 4, 16, 256), BF),
    pltpu.VMEM((2, 4, 4, 16, 256), BF),
    pltpu.VMEM((2, 4, 4, 16, 256), BF),
    pltpu.VMEM((7, 4, 16, 256), BF),
    pltpu.VMEM((2, 4, 16, 128), BF),
    pltpu.VMEM((15, 16, 128), BF),
    pltpu.SemaphoreType.DMA((2, 23)),
]
ROWS = pltpu.VMEM((TOK, D), BF)
SQUARE = pltpu.VMEM((D, D), BF)
RAW = pltpu.VMEM((6, 12, 4, D), BF)
PIECES = [pltpu.VMEM((2, 128, D), BF), pltpu.VMEM((2, 64, 256), BF), pltpu.VMEM((2, 4, 16, 256), BF)]
SEMS = pltpu.SemaphoreType.DMA((2, 4, 2))


def whole(
    sizes, factor, tok_in, cot_in, scale_in, wq_in, wk_in, wv_in, wo_in, down_in, up_in, pack_in, ends_in,
    main_out, tail_out, lora_out,
    raw_tok, raw_cot, scale, wq, wk, wv, wo, acat, ups, pack_table, ends, load, wide,
    main_tok, tail_tok, tails_tok, main_cot, tail_cot, tails_cot,
    send_tok, recv_tok, send_cot, recv_cot, send_out, recv_out,
    w_tok, w_cot, hs, q, k, v, da, at, dq, dk, dv, dh, tg, tg_tail, low, back, mean, rstd, bias,
    gt, r1, s1, r2, s2, r3, sems,
):
    reducer = Reducer()
    partners = ring_of(sizes) + reducer.partners()
    start_barrier(partners)
    moves = [
        (tok_in, raw_tok), (pack_in, pack_table), (cot_in, raw_cot), (ends_in, ends), (scale_in, scale),
        (down_in, acat), (up_in, ups), (wq_in, wq), (wk_in, wk), (wv_in, wv), (wo_in, wo),
    ]
    loads = [pltpu.make_async_copy(a, b, load.at[n]) for n, (a, b) in enumerate(moves)]
    for copy in loads:
        copy.start()
    weights = (wq, wk, wv, wo)

    loads[0].wait()
    natural_rows(raw_tok, wide)
    loads[1].wait()
    pack(wide, pack_table, main_tok, tail_tok)
    end_barrier(partners)
    tok_copies = in_copies(sizes, main_tok, tail_tok, w_tok, tails_tok, send_tok, recv_tok)
    for copy in tok_copies:
        copy.start()
    loads[2].wait()
    natural_rows(raw_cot, wide)
    pack(wide, pack_table, main_cot, tail_cot)
    cot_copies = in_copies(sizes, main_cot, tail_cot, w_cot, tails_cot, send_cot, recv_cot)
    for copy in cot_copies:
        copy.start()
    keep_own(main_tok, tail_tok, w_tok, tails_tok)
    keep_own(main_cot, tail_cot, w_cot, tails_cot)
    make_bias(sizes, bias)
    for copy in loads[3:]:
        copy.wait()
    for copy in tok_copies:
        copy.wait()
    for w in range(2):
        tails_to_window(ends, tails_tok[w], w_tok, WIN * w)
    norm_rows(w_tok, scale, hs, mean, rstd)
    project_tokens(hs, weights, ups, acat, low, q, k, v)
    for copy in cot_copies:
        copy.wait()
    for w in range(2):
        tails_to_window(ends, tails_cot[w], w_cot, WIN * w)
    project_cotangent(w_cot, wo, ups, acat, back, da)
    attend(q, k, v, da, bias, at, dq, dk, dv)
    lora_partials(hs, w_cot, at, dq, dk, dv, ups, acat, low, back, gt)
    first = reducer.start_first(gt, r1, sems)
    hidden_gradient((0, 1, 2), weights, dq, dk, dv, acat, back, dh)
    second = reducer.start_second(first, gt, r1, s1, r2, sems)
    hidden_gradient((3,), weights, dq, dk, dv, acat, back, dh)
    norm_gradient(w_tok, w_cot, scale, mean, rstd, dh, tg)
    for w in range(2):
        tg_tail[w] = window_to_tails(ends, tg[WIN * w + 128 : WIN * w + 144, :])
    out = out_copies(sizes, tg, tg_tail, main_out, tail_out, send_out, recv_out)
    for copy in out:
        copy.start()
    return_own(tg, tg_tail, main_out, tail_out)
    third = reducer.start_third(second, s1, r2, s2, r3, sems)
    for copy in out:
        copy.wait()
    reducer.finish(third, s2, r3, lora_out, factor)


def unpack(table, main, tail, lora, grad_out, down_out, up_out, wide):
    for ah in range(2):
        for k in range(4):
            cols = slice(256 * k, 256 * k + 256)
            wide[:, cols] = dot(table[0:144, 0:128], main[ah, :, cols]) + dot(
                table[144:288, 64 * k : 64 * k + 64], tail[ah]
            )
        for a in range(3):
            for o in range(12):
                row = (12 * a + o) * 4
                grad_out[3 * ah + a, o] = wide[row : row + 4, :].astype(BF)
    down_out[...] = lora[:, 0:32]
    up_out[...] = lora[:, 32:64]


def vmem(n):
    return [pl.BlockSpec(memory_space=pltpu.VMEM)] * n


def local(
    sizes, tokens, cotangent, norm_scale_vector, query_matrix, key_matrix, value_matrix, output_matrix,
    adapter_down_maps, adapter_up_maps,
):
    pack_table, unpack_table, ends = move_tables()
    factor = float(TOK * sizes["lon"] * sizes["lat"]) ** (-0.5)
    main, tail, lora = pl.pallas_call(
        functools.partial(whole, sizes, factor),
        out_shape=(
            jax.ShapeDtypeStruct((2, 128, D), BF),
            jax.ShapeDtypeStruct((2, 64, 256), BF),
            jax.ShapeDtypeStruct((16, 64), F32),
        ),
        in_specs=[pl.BlockSpec(memory_space=pl.ANY)] * 11,
        out_specs=tuple(vmem(3)),
        scratch_shapes=[
            RAW, RAW, pltpu.VMEM((8, 128), BF), SQUARE, SQUARE, SQUARE, SQUARE,
            pltpu.VMEM((128, D), BF), pltpu.VMEM((128, D), BF),
            pltpu.VMEM((384, 144), BF), pltpu.VMEM((128, 64), BF),
            pltpu.SemaphoreType.DMA((11,)), pltpu.VMEM((TOK, D), F32),
        ]
        + PIECES
        + PIECES
        + [SEMS] * 6
        + [ROWS] * 13
        + [
            pltpu.VMEM((2, 4, 16, 256), BF), pltpu.VMEM((TOK, 128), BF), pltpu.VMEM((TOK, 128), BF),
            pltpu.VMEM((TOK, 1), F32), pltpu.VMEM((TOK, 1), F32), pltpu.VMEM((2, WIN, 4 * WIN), F32),
        ]
        + REDUCE_SCRATCH,
        compiler_params=pltpu.CompilerParams(
            collective_id=0, has_side_effects=True, vmem_limit_bytes=VMEM_LIMIT
        ),
    )(
        tokens.transpose(1, 2, 0, 3), cotangent.transpose(1, 2, 0, 3), norm_scale_vector.reshape(8, 128),
        query_matrix, key_matrix, value_matrix, output_matrix,
        adapter_down_maps.transpose(0, 2, 1).reshape(128, D), adapter_up_maps.reshape(128, D), pack_table, ends,
    )
    grad, down, up = pl.pallas_call(
        unpack,
        out_shape=(
            jax.ShapeDtypeStruct((6, 12, 4, D), BF),
            jax.ShapeDtypeStruct((16, 32), F32),
            jax.ShapeDtypeStruct((16, 32), F32),
        ),
        in_specs=vmem(4),
        out_specs=tuple(vmem(3)),
        scratch_shapes=[pltpu.VMEM((WIN, D), F32)],
        compiler_params=pltpu.CompilerParams(vmem_limit_bytes=VMEM_LIMIT),
    )(unpack_table, main, tail, lora)
    return grad.transpose(2, 0, 1, 3), down, up.T


def solution(mesh):
    sizes = dict(mesh.shape)
    spread = P(None, "lat", "lon", None)
    return jax.shard_map(
        functools.partial(local, sizes),
        mesh=mesh,
        in_specs=(spread, spread, P(), P(), P(), P(), P(), P(), P()),
        out_specs=(spread, P(("lon", "lat"), None), P(None, ("lon", "lat"))),
        check_vma=False,
    )
```

```python
import functools

import jax
import jax.numpy as jnp
import numpy as np
from jax import lax
from jax.experimental import pallas as pl
from jax.experimental.pallas import tpu as pltpu
from jax.sharding import PartitionSpec as P

MESH = pl.DeviceIdType.MESH
BF = jnp.bfloat16
F32 = jnp.float32
EPS = 1e-05
NEG = -1e30
D = 1024
WIN = 144
TOK = 2 * WIN
LEVELS = ((1, 2), (3, 0))
OWN = (3, 0)
VMEM_LIMIT = 60 * 1024 * 1024


def move_tables():
    pack = np.zeros((384, 144), np.float32)
    unpack = np.zeros((288, 256), np.float32)
    ends = np.zeros((128, 64), np.float32)

    def source(w, h, t):
        return (t // 6 % 3) * 48 + (6 * h + t % 6) * 4 + LEVELS[w][t // 18]

    for w in range(2):
        for h in range(2):
            for t in range(32):
                row = 64 * w + 32 * h + t
                pack[row, source(w, h, t)] = 1
                unpack[source(w, h, t), row] = 1
            for k in range(4):
                for t in range(4):
                    row = 32 * w + 16 * h + 4 * k + t
                    pack[128 + 64 * k + row, source(w, h, 32 + t)] = 1
                    unpack[144 + source(w, h, 32 + t), 64 * k + row] = 1
    for p in range(4):
        for k in range(4):
            for t in range(4):
                ends[16 * k + 4 * p + t, 16 * p + 4 * k + t] = 1
                ends[64 + 16 * p + 4 * k + t, 16 * k + 4 * p + t] = 1
    return tuple(jnp.asarray(table, BF) for table in (pack, unpack, ends))


def dot(a, b):
    return jnp.dot(a, b, preferred_element_type=F32)


def dot_nt(a, b):
    return lax.dot_general(a, b, (((1,), (1,)), ((), ())), preferred_element_type=F32)


def dot_tn(a, b):
    return lax.dot_general(a, b, (((0,), (0,)), ((), ())), preferred_element_type=F32)


def neighbour(sizes, lat_step, lon_step):
    lon = lax.rem(lax.axis_index("lon") + lon_step + sizes["lon"], sizes["lon"])
    lat = lax.rem(lax.axis_index("lat") + lat_step + sizes["lat"], sizes["lat"])
    return (lon, lat)


def steps_of(w, p):
    differs = p ^ OWN[w]
    sign = -1 if w == 0 else 1
    return sign * (differs >> 1), sign * (differs & 1)


def moving_pieces():
    return [(w, p) for w in range(2) for p in range(4) if p != OWN[w]]


def ring_of(sizes):
    return [neighbour(sizes, *steps_of(w, p)) for w, p in moving_pieces()]


def remote(src, dst, send, recv, device):
    return pltpu.make_async_remote_copy(
        src_ref=src, dst_ref=dst, send_sem=send, recv_sem=recv, device_id=device, device_id_type=MESH
    )


def natural_rows(raw, wide):
    for a in range(6):
        for o in range(12):
            row = (12 * a + o) * 4
            wide[row : row + 4, :] = raw[a, o].astype(F32)


def piece_rows(w, p):
    return p >> 1, 64 * w + 32 * (p & 1)


def pack(natural, table, main, tail):
    for ah in range(2):
        rows = natural[WIN * ah : WIN * ah + WIN, :].astype(BF)
        main[ah] = dot(table[0:128, :], rows).astype(BF)
        ends = dot(table[128:192, :], rows[:, 0:256])
        for k in range(1, 4):
            ends = ends + dot(
                table[128 + 64 * k : 192 + 64 * k, :], rows[:, 256 * k : 256 * k + 256]
            )
        tail[ah] = ends.astype(BF)


def tails_to_window(table, tails, window, first):
    stacked = tails.reshape(64, 256)
    for k in range(4):
        window[first + 128 : first + 144, 256 * k : 256 * k + 256] = dot(
            table[16 * k : 16 * k + 16, :], stacked
        ).astype(BF)


def window_to_tails(table, rows):
    ends = jnp.zeros((64, 256), F32)
    for k in range(4):
        ends = ends + dot(
            table[64:128, 16 * k : 16 * k + 16], rows[:, 256 * k : 256 * k + 256]
        )
    return ends.astype(BF).reshape(4, 16, 256)


def in_copies(sizes, main, tail, window, tails, send, recv):
    copies = []
    for w, p in moving_pieces():
        device = neighbour(sizes, *steps_of(w, p))
        ah, row = piece_rows(w, p)
        copies.append(
            remote(
                main.at[ah, pl.ds(row, 32)], window.at[pl.ds(WIN * w + 32 * p, 32)],
                send.at[w, p, 0], recv.at[w, p, 0], device,
            )
        )
        copies.append(
            remote(
                tail.at[ah, pl.ds(row // 2, 16)], tails.at[w, p],
                send.at[w, p, 1], recv.at[w, p, 1], device,
            )
        )
    return copies


def keep_own(main, tail, window, tails):
    for w in range(2):
        p = OWN[w]
        ah, row = piece_rows(w, p)
        window[WIN * w + 32 * p : WIN * w + 32 * p + 32, :] = main[ah, row : row + 32]
        tails[w, p] = tail[ah, row // 2 : row // 2 + 16]


def out_copies(sizes, tg, tg_tail, main, tail, send, recv):
    copies = []
    for w, p in moving_pieces():
        lat_step, lon_step = steps_of(w, p)
        device = neighbour(sizes, -lat_step, -lon_step)
        ah, row = piece_rows(w, p)
        copies.append(
            remote(
                tg.at[pl.ds(WIN * w + 32 * p, 32)], main.at[ah, pl.ds(row, 32)],
                send.at[w, p, 0], recv.at[w, p, 0], device,
            )
        )
        copies.append(
            remote(
                tg_tail.at[w, p], tail.at[ah, pl.ds(row // 2, 16)],
                send.at[w, p, 1], recv.at[w, p, 1], device,
            )
        )
    return copies


def return_own(tg, tg_tail, main, tail):
    for w in range(2):
        p = OWN[w]
        ah, row = piece_rows(w, p)
        main[ah, row : row + 32] = tg[WIN * w + 32 * p : WIN * w + 32 * p + 32, :]
        tail[ah, row // 2 : row // 2 + 16] = tg_tail[w, p]


def start_barrier(devices):
    barrier = pltpu.get_barrier_semaphore()
    for device in devices:
        pl.semaphore_signal(barrier, inc=1, device_id=device, device_id_type=MESH)


def end_barrier(devices):
    pl.semaphore_wait(pltpu.get_barrier_semaphore(), len(devices))


def gain_of(scale):
    rows = scale[...].astype(F32)
    return jnp.concatenate([rows[n : n + 1] for n in range(8)], 1)


def slot_lanes(values, slots):
    lane = lax.broadcasted_iota(jnp.int32, values.shape, 1) // 32
    keep = lane == slots[0]
    for slot in slots[1:]:
        keep = keep | (lane == slot)
    return jnp.where(keep, values, 0.0)


def norm_rows(w_tok, scale, hs, mean, rstd):
    gain = gain_of(scale)

    def body(i, carry):
        rows = pl.ds(pl.multiple_of(i * 48, 48), 48)
        x = w_tok[rows, :].astype(F32)
        mu = jnp.mean(x, axis=-1, keepdims=True)
        center = x - mu
        inverse = lax.rsqrt(jnp.mean(center * center, axis=-1, keepdims=True) + EPS)
        mean[rows, :] = mu
        rstd[rows, :] = inverse
        hs[rows, :] = (center * inverse * gain).astype(BF)
        return carry

    lax.fori_loop(0, TOK // 48, body, 0, unroll=2)


def project_tokens(hs, weights, ups, acat, low, q, k, v):
    low[...] = dot_nt(hs[...], acat[...]).astype(BF)
    lows = [slot_lanes(low[...].astype(F32), (n,)).astype(BF) for n in range(3)]
    for c in range(4):
        cols = slice(256 * c, 256 * c + 256)
        for n, (w, out) in enumerate(zip(weights[:3], (q, k, v))):
            out[:, cols] = (dot(hs[...], w[:, cols]) + dot(lows[n], ups[:, cols])).astype(BF)


def project_cotangent(w_cot, wo, ups, acat, back, da):
    back[...] = slot_lanes(dot_nt(w_cot[...], ups[...]), (3,)).astype(BF)
    for c in range(4):
        cols = slice(256 * c, 256 * c + 256)
        da[:, cols] = (dot_nt(w_cot[...], wo[cols, :]) + dot(back[...], acat[:, cols])).astype(BF)


def make_bias(sizes, bias):
    lat = lax.axis_index("lat")

    def coordinates(r):
        tail = r >= 128
        piece = jnp.where(tail, (r - 128) // 4, r // 32)
        t = jnp.where(tail, 32 + r % 4, r % 32)
        return (piece < 2).astype(jnp.int32), (t >= 18).astype(jnp.int32)

    key_ah, key_lv = coordinates(lax.broadcasted_iota(jnp.int32, (WIN, 4 * WIN), 0))
    c = lax.broadcasted_iota(jnp.int32, (WIN, 4 * WIN), 1)
    for n in (3, 2, 1):
        c = jnp.where(c >= n * WIN, c - n * WIN, c)
    query_ah, query_lv = coordinates(c)
    for w in range(2):
        last = (lat == (sizes["lat"] - 1 if w == 0 else 0)).astype(jnp.int32)
        differs = (key_ah != query_ah).astype(jnp.int32) * last
        if w == 1:
            differs = differs + (key_lv != query_lv).astype(jnp.int32)
        bias[w] = jnp.where(differs > 0, NEG, 0.0).astype(F32)


def attend(q, k, v, da, bias, at, dq, dk, dv):
    lane = lax.broadcasted_iota(jnp.int32, (1, 256), 1) // 64
    masks = [(lane == h).astype(F32).astype(BF) for h in range(4)]
    lanes = lax.broadcasted_iota(jnp.int32, (WIN, 256), 1) // 64

    def stacked(values):
        return jnp.concatenate([values * mask for mask in masks], 0)

    def own_blocks(values):
        result = values[0:WIN]
        for h in range(1, 4):
            result = jnp.where(lanes == h, values[WIN * h : WIN * h + WIN], result)
        return result

    def body(c, carry):
        cols = pl.ds(pl.multiple_of(c * 256, 256), 256)
        for w in range(2):
            rows = pl.ds(WIN * w, WIN)
            kk = k[rows, cols]
            vv = v[rows, cols]
            q4 = stacked(q[rows, cols] * jnp.asarray(0.125, BF))
            d4 = stacked(da[rows, cols])
            s = dot_nt(kk, q4) + bias[w]
            e = jnp.exp(s - jnp.max(s, axis=0, keepdims=True))
            p = e * (1.0 / jnp.sum(e, axis=0, keepdims=True))
            dp = dot_nt(vv, d4)
            ds = (p * (dp - jnp.sum(dp * p, axis=0, keepdims=True))).astype(BF)
            pb = p.astype(BF)
            dv[rows, cols] = dot(pb, d4).astype(BF)
            dk[rows, cols] = dot(ds, q4).astype(BF)
            at[rows, cols] = own_blocks(dot_tn(pb, vv)).astype(BF)
            dq[rows, cols] = (own_blocks(dot_tn(ds, kk)) * 0.125).astype(BF)
        return carry

    lax.fori_loop(0, 4, body, 0)


def adapter_sides(w_cot, at, dq, dk, dv, ups, acat, low, back):
    lane = lax.broadcasted_iota(jnp.int32, (TOK, 128), 1) // 32
    backs = back[...].astype(F32)
    for n, d in enumerate((dq, dk, dv)):
        backs = jnp.where(lane == n, dot_nt(d[...], ups[...]), backs)
    back[...] = backs.astype(BF)
    lows = jnp.where(lane == 3, dot_nt(at[...], acat[...]), low[...].astype(F32))
    return backs.T.astype(BF), lows.T.astype(BF)


def lora_partials(z1, sides, hs, w_cot, at, dq, dk, dv, gt):
    back_t, low_t = sides
    for z0 in range(2):
        c = 2 * z1 + z0
        cols = slice(256 * c, 256 * c + 256)
        own_down = dot(back_t[0:96], hs[:, cols])
        last_down = dot(back_t[96:128], at[:, cols])
        ups_own = [dot(low_t[32 * n : 32 * n + 32], d[:, cols]) for n, d in enumerate((dq, dk, dv, w_cot))]
        parts = []
        for n in range(4):
            parts.append(own_down[32 * n : 32 * n + 32] if n < 3 else last_down)
            parts.append(ups_own[n])
        block = jnp.concatenate(parts, 0)
        for half in range(2):
            turned = block[:, 128 * half : 128 * half + 128].T.astype(BF)
            for b in range(8):
                y, lat = 2 * half + b // 4, b % 4
                rows = turned[16 * b : 16 * b + 16]
                for xh in range(2):
                    gt[lat % 2, z1, xh, lat // 2, y, z0] = rows[:, 128 * xh : 128 * xh + 128]


def hidden_gradient(chunks, weights, dq, dk, dv, acat, back, dh):
    backs = slot_lanes(back[...].astype(F32), (0, 1, 2)).astype(BF)
    for c in chunks:
        cols = slice(256 * c, 256 * c + 256)
        total = dot(backs, acat[:, cols])
        for w, d in zip(weights[:3], (dq, dk, dv)):
            total = total + dot_nt(d[...], w[cols, :])
        dh[:, cols] = total.astype(BF)


def norm_gradient(w_tok, w_cot, scale, mean, rstd, dh, tg):
    gain = gain_of(scale)

    def body(i, carry):
        rows = pl.ds(pl.multiple_of(i * 48, 48), 48)
        inverse = rstd[rows, :]
        xhat = (w_tok[rows, :].astype(F32) - mean[rows, :]) * inverse
        g = dh[rows, :].astype(F32) * gain
        first = jnp.mean(g, axis=-1, keepdims=True)
        second = jnp.mean(g * xhat, axis=-1, keepdims=True)
        tg[rows, :] = (w_cot[rows, :].astype(F32) + inverse * (g - first - xhat * second)).astype(BF)
        return carry

    lax.fori_loop(0, TOK // 48, body, 0, unroll=2)


class Reducer:
    def __init__(self):
        lon = lax.axis_index("lon")
        lat = lax.axis_index("lat")
        y = lax.rem(lon, 4)
        z = lax.rem(lon // 4, 8)
        xh, xl, core = lon // 32, lat // 2, lax.rem(lat, 2)
        self.core, self.z = core, z
        self.mine = (xh, xl, y)

        def device(xh, z, y, xl, core):
            return ((xh * 8 + z) * 4 + y, xl * 2 + core)

        self.first = device(xh, z, y, xl, 1 - core)
        self.second = []
        for n in range(1, 16):
            to = lax.rem(xh + n // 8, 2), lax.rem(xl + n // 4, 2), lax.rem(y + n, 4)
            self.second.append((n - 1, to, device(to[0], z, to[2], to[1], core)))
        self.third = []
        for n in range(1, 8):
            to = lax.rem(z + n, 8)
            self.third.append((n - 1, to, device(xh, to, y, xl, core)))

    def partners(self):
        return [self.first] + [s[-1] for s in self.second] + [s[-1] for s in self.third]

    def start_first(self, part, gt, r1, sems):
        copy = remote(gt.at[1 - self.core, part], r1.at[part], sems.at[0, part], sems.at[1, part], self.first)
        copy.start()
        return copy

    def start_second(self, part, copy, gt, r1, s1, r2, sems):
        copy.wait()
        s1[part] = (gt[self.core, part].astype(F32) + r1[part].astype(F32)).astype(BF)
        copies = []
        for n, to, device in self.second:
            sem = 2 + 15 * part + n
            copies.append(
                remote(s1.at[part, to[0], to[1], to[2]], r2.at[part, n], sems.at[0, sem], sems.at[1, sem], device)
            )
            copies[-1].start()
        return copies

    def sum_second(self, part, copies, s1, r2, s2):
        total = s1[part, self.mine[0], self.mine[1], self.mine[2]].astype(F32)
        for copy in copies:
            copy.wait()
        for n in range(15):
            total = total + r2[part, n].astype(F32)
        s2[part] = total.astype(BF)

    def start_third(self, s2, r3, sems):
        copies = []
        for n, to, device in self.third:
            sem = 32 + n
            block = s2.at[lax.rem(to // 2, 2), lax.rem(to, 2)]
            copies.append(remote(block, r3.at[n], sems.at[0, sem], sems.at[1, sem], device))
            copies[-1].start()
        return copies

    def finish(self, copies, s2, r3, down_out, up_out, factor):
        total = s2[lax.rem(self.z // 2, 2), lax.rem(self.z, 2)].astype(F32)
        for copy in copies:
            copy.wait()
        for n in range(7):
            total = total + r3[n].astype(F32)
        total = total * factor
        total = jnp.where(self.z < 4, total[:, 0:64], total[:, 64:128])
        down_out[...] = total[:, 0:32]
        up_out[...] = total[:, 32:64]


REDUCE_SCRATCH = [
    pltpu.VMEM((2, 2, 2, 2, 4, 2, 16, 128), BF),
    pltpu.VMEM((2, 2, 2, 4, 2, 16, 128), BF),
    pltpu.VMEM((2, 2, 2, 4, 2, 16, 128), BF),
    pltpu.VMEM((2, 15, 2, 16, 128), BF),
    pltpu.VMEM((2, 2, 16, 128), BF),
    pltpu.VMEM((7, 16, 128), BF),
    pltpu.SemaphoreType.DMA((2, 39)),
]
ROWS = pltpu.VMEM((TOK, D), BF)
WIDE = pltpu.VMEM((TOK, D), F32)
SQUARE = pltpu.VMEM((D, D), BF)
RAW = pltpu.VMEM((6, 12, 4, D), BF)
PIECES = [pltpu.VMEM((2, 128, D), BF), pltpu.VMEM((2, 64, 256), BF)]
TAILS = pltpu.VMEM((2, 4, 16, 256), BF)
SEMS = pltpu.SemaphoreType.DMA((2, 4, 2))


def whole(
    sizes, factor, tok_in, cot_in, scale_in, wq_in, wk_in, wv_in, wo_in, down_in, up_in, pack_in, ends_in,
    main_back, tail_back, down_out, up_out,
    raw_tok, raw_cot, scale, wq, wk, wv, wo, acat, ups, pack_table, ends, load, wide,
    main_tok, tail_tok, main_cot, tail_cot, tails_tok, tails_cot, tails_out,
    send_tok, recv_tok, send_cot, recv_cot, send_out, recv_out,
    w_tok, w_cot, hs, q, k, v, da, at, dq, dk, dv, dh, tg, low, back, mean, rstd, bias,
    gt, r1, s1, r2, s2, r3, sems,
):
    reducer = Reducer()
    partners = ring_of(sizes) + reducer.partners()
    start_barrier(partners)
    moves = [
        (tok_in, raw_tok), (pack_in, pack_table), (cot_in, raw_cot), (ends_in, ends), (scale_in, scale),
        (down_in, acat), (up_in, ups), (wq_in, wq), (wk_in, wk), (wv_in, wv), (wo_in, wo),
    ]
    loads = [pltpu.make_async_copy(a, b, load.at[n]) for n, (a, b) in enumerate(moves)]
    for copy in loads[:3]:
        copy.start()
    weights = (wq, wk, wv, wo)

    loads[0].wait()
    for copy in loads[3:]:
        copy.start()
    natural_rows(raw_tok, wide)
    loads[1].wait()
    pack(wide, pack_table, main_tok, tail_tok)
    end_barrier(partners)
    tok_copies = in_copies(sizes, main_tok, tail_tok, w_tok, tails_tok, send_tok, recv_tok)
    for copy in tok_copies:
        copy.start()
    keep_own(main_tok, tail_tok, w_tok, tails_tok)
    loads[2].wait()
    natural_rows(raw_cot, wide)
    pack(wide, pack_table, main_cot, tail_cot)
    keep_own(main_cot, tail_cot, w_cot, tails_cot)
    make_bias(sizes, bias)
    for copy in tok_copies:
        copy.wait_send()
    cot_copies = in_copies(sizes, main_cot, tail_cot, w_cot, tails_cot, send_cot, recv_cot)
    for copy in cot_copies:
        copy.start()
    for copy in loads[3:]:
        copy.wait()
    for copy in tok_copies:
        copy.wait_recv()
    for w in range(2):
        tails_to_window(ends, tails_tok[w], w_tok, WIN * w)
    norm_rows(w_tok, scale, hs, mean, rstd)
    project_tokens(hs, weights, ups, acat, low, q, k, v)
    for copy in cot_copies:
        copy.wait()
    for w in range(2):
        tails_to_window(ends, tails_cot[w], w_cot, WIN * w)
    project_cotangent(w_cot, wo, ups, acat, back, da)
    attend(q, k, v, da, bias, at, dq, dk, dv)
    sides = adapter_sides(w_cot, at, dq, dk, dv, ups, acat, low, back)
    first = []
    for part in range(2):
        lora_partials(part, sides, hs, w_cot, at, dq, dk, dv, gt)
        first.append(reducer.start_first(part, gt, r1, sems))
    hidden_gradient((0,), weights, dq, dk, dv, acat, back, dh)
    second = [reducer.start_second(part, first[part], gt, r1, s1, r2, sems) for part in range(2)]
    hidden_gradient((1, 2, 3), weights, dq, dk, dv, acat, back, dh)
    norm_gradient(w_tok, w_cot, scale, mean, rstd, dh, tg)
    for w in range(2):
        tails_out[w] = window_to_tails(ends, tg[WIN * w + 128 : WIN * w + 144, :])
    out = out_copies(sizes, tg, tails_out, main_back, tail_back, send_out, recv_out)
    for copy in out:
        copy.start()
    return_own(tg, tails_out, main_back, tail_back)
    for part in range(2):
        reducer.sum_second(part, second[part], s1, r2, s2)
    third = reducer.start_third(s2, r3, sems)
    for copy in out:
        copy.wait()
    reducer.finish(third, s2, r3, down_out, up_out, factor)


def unpack(table, main, tail, down, up, grad_out, down_out, up_out, wide):
    for ah in range(2):
        for k in range(4):
            cols = slice(256 * k, 256 * k + 256)
            wide[:, cols] = dot(table[0:144, 0:128], main[ah, :, cols]) + dot(
                table[144:288, 64 * k : 64 * k + 64], tail[ah]
            )
        for a in range(3):
            for o in range(12):
                row = (12 * a + o) * 4
                grad_out[3 * ah + a, o] = wide[row : row + 4, :].astype(BF)
    down_out[...] = down[...]
    up_out[...] = up[...]


def vmem(n):
    return [pl.BlockSpec(memory_space=pltpu.VMEM)] * n


def local(
    sizes, tokens, cotangent, norm_scale_vector, query_matrix, key_matrix, value_matrix, output_matrix,
    adapter_down_maps, adapter_up_maps,
):
    pack_table, unpack_table, ends = move_tables()
    factor = float(TOK * sizes["lon"] * sizes["lat"]) ** (-0.5)
    anywhere = pl.BlockSpec(memory_space=pl.ANY)
    results = (
        jax.ShapeDtypeStruct((6, 12, 4, D), BF),
        jax.ShapeDtypeStruct((16, 32), F32),
        jax.ShapeDtypeStruct((16, 32), F32),
    )
    made = pl.pallas_call(
        functools.partial(whole, sizes, factor),
        out_shape=(
            jax.ShapeDtypeStruct((2, 128, D), BF), jax.ShapeDtypeStruct((2, 64, 256), BF), *results[1:],
        ),
        in_specs=[anywhere] * 11,
        out_specs=tuple(vmem(4)),
        scratch_shapes=[
            RAW, RAW, pltpu.VMEM((8, 128), BF), SQUARE, SQUARE, SQUARE, SQUARE,
            pltpu.VMEM((128, D), BF), pltpu.VMEM((128, D), BF),
            pltpu.VMEM((384, 144), BF), pltpu.VMEM((128, 64), BF), pltpu.SemaphoreType.DMA((11,)), WIDE,
        ]
        + PIECES * 2
        + [TAILS] * 3
        + [SEMS] * 6
        + [ROWS] * 13
        + [
            pltpu.VMEM((TOK, 128), BF), pltpu.VMEM((TOK, 128), BF),
            pltpu.VMEM((TOK, 1), F32), pltpu.VMEM((TOK, 1), F32), pltpu.VMEM((2, WIN, 4 * WIN), F32),
        ]
        + REDUCE_SCRATCH,
        compiler_params=pltpu.CompilerParams(
            collective_id=0, has_side_effects=True, vmem_limit_bytes=VMEM_LIMIT
        ),
    )(
        tokens.transpose(1, 2, 0, 3), cotangent.transpose(1, 2, 0, 3), norm_scale_vector.reshape(8, 128),
        query_matrix, key_matrix, value_matrix, output_matrix,
        adapter_down_maps.transpose(0, 2, 1).reshape(128, D), adapter_up_maps.reshape(128, D),
        pack_table, ends,
    )
    grad, down, up = pl.pallas_call(
        unpack,
        out_shape=results,
        in_specs=vmem(5),
        out_specs=tuple(vmem(3)),
        scratch_shapes=[pltpu.VMEM((WIN, D), F32)],
        compiler_params=pltpu.CompilerParams(vmem_limit_bytes=VMEM_LIMIT),
    )(unpack_table, *made)
    return grad.transpose(2, 0, 1, 3), down, up.T


def solution(mesh):
    sizes = dict(mesh.shape)
    spread = P(None, "lat", "lon", None)
    return jax.shard_map(
        functools.partial(local, sizes),
        mesh=mesh,
        in_specs=(spread, spread, P(), P(), P(), P(), P(), P(), P()),
        out_specs=(spread, P(("lon", "lat"), None), P(None, ("lon", "lat"))),
        check_vma=False,
    )
```

```python
import functools

import jax
import jax.numpy as jnp
import numpy as np
from jax import lax
from jax.experimental import pallas as pl
from jax.experimental.pallas import tpu as pltpu
from jax.sharding import PartitionSpec as P

MESH = pl.DeviceIdType.MESH
BF = jnp.bfloat16
F32 = jnp.float32
EPS = 1e-05
NEG = -1e30
D = 1024
WIN = 144
TOK = 2 * WIN
LEVELS = ((1, 2), (3, 0))
OWN = (3, 0)
VMEM_LIMIT = 60 * 1024 * 1024


def move_tables():
    pack = np.zeros((4, 192, 144), np.float32)
    unpack = np.zeros((4, 144, 192), np.float32)
    ends = np.zeros((128, 64), np.float32)

    def source(w, h, t):
        return (t // 6 % 3) * 48 + (6 * h + t % 6) * 4 + LEVELS[w][t // 18]

    for w in range(2):
        for h in range(2):
            for t in range(32):
                row = 64 * w + 32 * h + t
                pack[:, row, source(w, h, t)] = 1
                unpack[:, source(w, h, t), row] = 1
            for k in range(4):
                for t in range(4):
                    row = 128 + 32 * w + 16 * h + 4 * k + t
                    pack[k, row, source(w, h, 32 + t)] = 1
                    unpack[k, source(w, h, 32 + t), row] = 1
    for p in range(4):
        for k in range(4):
            for t in range(4):
                ends[16 * k + 4 * p + t, 16 * p + 4 * k + t] = 1
                ends[64 + 16 * p + 4 * k + t, 16 * k + 4 * p + t] = 1
    return tuple(jnp.asarray(table, BF) for table in (pack, unpack, ends))


def dot(a, b):
    return jnp.dot(a, b, preferred_element_type=F32)


def dot_nt(a, b):
    return lax.dot_general(a, b, (((1,), (1,)), ((), ())), preferred_element_type=F32)


def dot_tn(a, b):
    return lax.dot_general(a, b, (((0,), (0,)), ((), ())), preferred_element_type=F32)


def neighbour(sizes, lat_step, lon_step):
    lon = lax.rem(lax.axis_index("lon") + lon_step + sizes["lon"], sizes["lon"])
    lat = lax.rem(lax.axis_index("lat") + lat_step + sizes["lat"], sizes["lat"])
    return (lon, lat)


def steps_of(w, p):
    differs = p ^ OWN[w]
    sign = -1 if w == 0 else 1
    return sign * (differs >> 1), sign * (differs & 1)


def moving_pieces():
    return [(w, OWN[w] ^ differs) for differs in (3, 1, 2) for w in range(2)]


def ring_of(sizes):
    return [neighbour(sizes, *steps_of(w, p)) for w, p in moving_pieces()]


def remote(src, dst, send, recv, device):
    return pltpu.make_async_remote_copy(
        src_ref=src, dst_ref=dst, send_sem=send, recv_sem=recv, device_id=device, device_id_type=MESH
    )


def natural_rows(raw, wide):
    for a in range(6):
        for o in range(12):
            row = (12 * a + o) * 4
            wide[row : row + 4, :] = raw[a, o].astype(F32)


def piece_rows(w, p):
    return p >> 1, 64 * w + 32 * (p & 1)


def pack(natural, table, main, tail):
    for ah in range(2):
        rows = natural[WIN * ah : WIN * ah + WIN, :].astype(BF)
        ends = jnp.zeros((64, 256), F32)
        for k in range(4):
            cols = slice(256 * k, 256 * k + 256)
            moved = dot(table[k], rows[:, cols])
            main[ah, :, cols] = moved[0:128].astype(BF)
            ends = ends + moved[128:192]
        tail[ah] = ends.astype(BF)


def tails_to_window(table, tails, window, first):
    stacked = tails.reshape(64, 256)
    for k in range(4):
        window[first + 128 : first + 144, 256 * k : 256 * k + 256] = dot(
            table[16 * k : 16 * k + 16, :], stacked
        ).astype(BF)


def window_to_tails(table, rows):
    ends = jnp.zeros((64, 256), F32)
    for k in range(4):
        ends = ends + dot(
            table[64:128, 16 * k : 16 * k + 16], rows[:, 256 * k : 256 * k + 256]
        )
    return ends.astype(BF).reshape(4, 16, 256)


def in_copies(sizes, main, tail, window, tails, send, recv):
    copies = []
    for w, p in moving_pieces():
        device = neighbour(sizes, *steps_of(w, p))
        ah, row = piece_rows(w, p)
        copies.append(
            remote(
                main.at[ah, pl.ds(row, 32)], window.at[pl.ds(WIN * w + 32 * p, 32)],
                send.at[w, p, 0], recv.at[w, p, 0], device,
            )
        )
        copies.append(
            remote(
                tail.at[ah, pl.ds(row // 2, 16)], tails.at[w, p],
                send.at[w, p, 1], recv.at[w, p, 1], device,
            )
        )
    return copies


def keep_own(main, tail, window, tails):
    for w in range(2):
        p = OWN[w]
        ah, row = piece_rows(w, p)
        window[WIN * w + 32 * p : WIN * w + 32 * p + 32, :] = main[ah, row : row + 32]
        tails[w, p] = tail[ah, row // 2 : row // 2 + 16]


def out_copies(sizes, tg, tg_tail, main, tail, send, recv):
    copies = []
    for w, p in moving_pieces():
        lat_step, lon_step = steps_of(w, p)
        device = neighbour(sizes, -lat_step, -lon_step)
        ah, row = piece_rows(w, p)
        copies.append(
            remote(
                tg.at[pl.ds(WIN * w + 32 * p, 32)], main.at[ah, pl.ds(row, 32)],
                send.at[w, p, 0], recv.at[w, p, 0], device,
            )
        )
        copies.append(
            remote(
                tg_tail.at[w, p], tail.at[ah, pl.ds(row // 2, 16)],
                send.at[w, p, 1], recv.at[w, p, 1], device,
            )
        )
    return copies


def return_own(tg, tg_tail, main, tail):
    for w in range(2):
        p = OWN[w]
        ah, row = piece_rows(w, p)
        main[ah, row : row + 32] = tg[WIN * w + 32 * p : WIN * w + 32 * p + 32, :]
        tail[ah, row // 2 : row // 2 + 16] = tg_tail[w, p]


def start_barrier(devices):
    barrier = pltpu.get_barrier_semaphore()
    for device in devices:
        pl.semaphore_signal(barrier, inc=1, device_id=device, device_id_type=MESH)


def end_barrier(devices):
    pl.semaphore_wait(pltpu.get_barrier_semaphore(), len(devices))


def gain_of(scale):
    rows = scale[...].astype(F32)
    return jnp.concatenate([rows[n : n + 1] for n in range(8)], 1)


def slot_lanes(values, slots):
    lane = lax.broadcasted_iota(jnp.int32, values.shape, 1) // 32
    keep = lane == slots[0]
    for slot in slots[1:]:
        keep = keep | (lane == slot)
    return jnp.where(keep, values, 0.0)


def norm_rows(w_tok, scale, hs, mean, rstd):
    gain = gain_of(scale)

    def body(i, carry):
        rows = pl.ds(pl.multiple_of(i * 48, 48), 48)
        x = w_tok[rows, :].astype(F32)
        mu = jnp.mean(x, axis=-1, keepdims=True)
        center = x - mu
        inverse = lax.rsqrt(jnp.mean(center * center, axis=-1, keepdims=True) + EPS)
        mean[rows, :] = mu
        rstd[rows, :] = inverse
        hs[rows, :] = (center * inverse * gain).astype(BF)
        return carry

    lax.fori_loop(0, TOK // 48, body, 0, unroll=2)


def project_tokens(hs, weights, ups, acat, low, q, k, v):
    low[...] = dot_nt(hs[...], acat[...]).astype(BF)
    lows = [slot_lanes(low[...].astype(F32), (n,)).astype(BF) for n in range(3)]
    for c in range(4):
        cols = slice(256 * c, 256 * c + 256)
        for n, (w, out) in enumerate(zip(weights[:3], (q, k, v))):
            out[:, cols] = (dot(hs[...], w[:, cols]) + dot(lows[n], ups[:, cols])).astype(BF)


def project_cotangent(w_cot, wo, ups, acat, back, da):
    back[...] = slot_lanes(dot_nt(w_cot[...], ups[...]), (3,)).astype(BF)
    for c in range(4):
        cols = slice(256 * c, 256 * c + 256)
        da[:, cols] = (dot_nt(w_cot[...], wo[cols, :]) + dot(back[...], acat[:, cols])).astype(BF)


def make_bias(sizes, bias):
    lat = lax.axis_index("lat")

    def coordinates(r):
        tail = r >= 128
        piece = jnp.where(tail, (r - 128) // 4, r // 32)
        t = jnp.where(tail, 32 + r % 4, r % 32)
        return (piece < 2).astype(jnp.int32), (t >= 18).astype(jnp.int32)

    key_ah, key_lv = coordinates(lax.broadcasted_iota(jnp.int32, (WIN, 4 * WIN), 0))
    c = lax.broadcasted_iota(jnp.int32, (WIN, 4 * WIN), 1)
    for n in (3, 2, 1):
        c = jnp.where(c >= n * WIN, c - n * WIN, c)
    query_ah, query_lv = coordinates(c)
    for w in range(2):
        last = (lat == (sizes["lat"] - 1 if w == 0 else 0)).astype(jnp.int32)
        differs = (key_ah != query_ah).astype(jnp.int32) * last
        if w == 1:
            differs = differs + (key_lv != query_lv).astype(jnp.int32)
        bias[w] = jnp.where(differs > 0, NEG, 0.0).astype(F32)


def attend(q, k, v, da, bias, at, dq, dk, dv):
    lane = lax.broadcasted_iota(jnp.int32, (1, 256), 1) // 64
    masks = [(lane == h).astype(F32).astype(BF) for h in range(4)]
    lanes = lax.broadcasted_iota(jnp.int32, (WIN, 256), 1) // 64

    def stacked(values):
        return jnp.concatenate([values * mask for mask in masks], 0)

    def own_blocks(values):
        result = values[0:WIN]
        for h in range(1, 4):
            result = jnp.where(lanes == h, values[WIN * h : WIN * h + WIN], result)
        return result

    def body(c, carry):
        cols = pl.ds(pl.multiple_of(c * 256, 256), 256)
        for w in range(2):
            rows = pl.ds(WIN * w, WIN)
            kk = k[rows, cols]
            vv = v[rows, cols]
            q4 = stacked(q[rows, cols] * jnp.asarray(0.125, BF))
            d4 = stacked(da[rows, cols])
            s = dot_nt(kk, q4) + bias[w]
            e = jnp.exp(s - jnp.max(s, axis=0, keepdims=True))
            p = e * (1.0 / jnp.sum(e, axis=0, keepdims=True))
            dp = dot_nt(vv, d4)
            ds = (p * (dp - jnp.sum(dp * p, axis=0, keepdims=True))).astype(BF)
            pb = p.astype(BF)
            dv[rows, cols] = dot(pb, d4).astype(BF)
            dk[rows, cols] = dot(ds, q4).astype(BF)
            at[rows, cols] = own_blocks(dot_tn(pb, vv)).astype(BF)
            dq[rows, cols] = (own_blocks(dot_tn(ds, kk)) * 0.125).astype(BF)
        return carry

    lax.fori_loop(0, 4, body, 0, unroll=2)


def adapter_sides(w_cot, at, dq, dk, dv, ups, acat, low, back):
    lane = lax.broadcasted_iota(jnp.int32, (TOK, 128), 1) // 32
    backs = back[...].astype(F32)
    for n, d in enumerate((dq, dk, dv)):
        backs = jnp.where(lane == n, dot_nt(d[...], ups[...]), backs)
    back[...] = backs.astype(BF)
    lows = jnp.where(lane == 3, dot_nt(at[...], acat[...]), low[...].astype(F32))
    return backs.T.astype(BF), lows.T.astype(BF)


def lora_partials(z1, sides, hs, w_cot, at, dq, dk, dv, gt):
    back_t, low_t = sides
    for z0 in range(2):
        c = 2 * z1 + z0
        cols = slice(256 * c, 256 * c + 256)
        own_down = dot(back_t[0:96], hs[:, cols])
        last_down = dot(back_t[96:128], at[:, cols])
        ups_own = [dot(low_t[32 * n : 32 * n + 32], d[:, cols]) for n, d in enumerate((dq, dk, dv, w_cot))]
        parts = []
        for n in range(4):
            parts.append(own_down[32 * n : 32 * n + 32] if n < 3 else last_down)
            parts.append(ups_own[n])
        block = jnp.concatenate(parts, 0)
        for half in range(2):
            turned = block[:, 128 * half : 128 * half + 128].T.astype(BF)
            for b in range(8):
                y, lat = 2 * half + b // 4, b % 4
                rows = turned[16 * b : 16 * b + 16]
                for xh in range(2):
                    gt[lat % 2, z1, xh, lat // 2, y, z0] = rows[:, 128 * xh : 128 * xh + 128]


def hidden_gradient(chunks, weights, dq, dk, dv, acat, back, dh):
    backs = slot_lanes(back[...].astype(F32), (0, 1, 2)).astype(BF)
    for c in chunks:
        cols = slice(256 * c, 256 * c + 256)
        total = dot(backs, acat[:, cols])
        for w, d in zip(weights[:3], (dq, dk, dv)):
            total = total + dot_nt(d[...], w[cols, :])
        dh[:, cols] = total.astype(BF)


def norm_gradient(w_tok, w_cot, scale, mean, rstd, dh, tg):
    gain = gain_of(scale)

    def body(i, carry):
        rows = pl.ds(pl.multiple_of(i * 48, 48), 48)
        inverse = rstd[rows, :]
        xhat = (w_tok[rows, :].astype(F32) - mean[rows, :]) * inverse
        g = dh[rows, :].astype(F32) * gain
        first = jnp.mean(g, axis=-1, keepdims=True)
        second = jnp.mean(g * xhat, axis=-1, keepdims=True)
        tg[rows, :] = (w_cot[rows, :].astype(F32) + inverse * (g - first - xhat * second)).astype(BF)
        return carry

    lax.fori_loop(0, TOK // 48, body, 0, unroll=2)


class Reducer:
    def __init__(self):
        lon = lax.axis_index("lon")
        lat = lax.axis_index("lat")
        y = lax.rem(lon, 4)
        z = lax.rem(lon // 4, 8)
        xh, xl, core = lon // 32, lat // 2, lax.rem(lat, 2)
        self.core, self.z = core, z
        self.mine = (xh, xl, y)

        def device(xh, z, y, xl, core):
            return ((xh * 8 + z) * 4 + y, xl * 2 + core)

        self.first = device(xh, z, y, xl, 1 - core)
        self.second = []
        for n in range(1, 16):
            to = lax.rem(xh + n // 8, 2), lax.rem(xl + n // 4, 2), lax.rem(y + n, 4)
            self.second.append((n - 1, to, device(to[0], z, to[2], to[1], core)))
        self.third = []
        for n in range(1, 8):
            to = lax.rem(z + n, 8)
            self.third.append((n - 1, to, device(xh, to, y, xl, core)))

    def partners(self):
        return [self.first] + [s[-1] for s in self.second] + [s[-1] for s in self.third]

    def start_first(self, part, gt, r1, sems):
        copy = remote(gt.at[1 - self.core, part], r1.at[part], sems.at[0, part], sems.at[1, part], self.first)
        copy.start()
        return copy

    def start_second(self, part, copy, gt, r1, s1, r2, sems):
        copy.wait()
        s1[part] = (gt[self.core, part].astype(F32) + r1[part].astype(F32)).astype(BF)
        copies = []
        for n, to, device in self.second:
            sem = 2 + 15 * part + n
            copies.append(
                remote(s1.at[part, to[0], to[1], to[2]], r2.at[part, n], sems.at[0, sem], sems.at[1, sem], device)
            )
            copies[-1].start()
        return copies

    def sum_second(self, part, copies, s1, r2, s2):
        total = s1[part, self.mine[0], self.mine[1], self.mine[2]].astype(F32)
        for copy in copies:
            copy.wait()
        for n in range(15):
            total = total + r2[part, n].astype(F32)
        s2[part] = total.astype(BF)

    def start_third(self, s2, r3, sems):
        copies = []
        for n, to, device in self.third:
            sem = 32 + n
            block = s2.at[lax.rem(to // 2, 2), lax.rem(to, 2)]
            copies.append(remote(block, r3.at[n], sems.at[0, sem], sems.at[1, sem], device))
            copies[-1].start()
        return copies

    def finish(self, copies, s2, r3, down_out, up_out, factor):
        total = s2[lax.rem(self.z // 2, 2), lax.rem(self.z, 2)].astype(F32)
        for copy in copies:
            copy.wait()
        for n in range(7):
            total = total + r3[n].astype(F32)
        total = total * factor
        total = jnp.where(self.z < 4, total[:, 0:64], total[:, 64:128])
        down_out[...] = total[:, 0:32]
        up_out[...] = total[:, 32:64]


REDUCE_SCRATCH = [
    pltpu.VMEM((2, 2, 2, 2, 4, 2, 16, 128), BF),
    pltpu.VMEM((2, 2, 2, 4, 2, 16, 128), BF),
    pltpu.VMEM((2, 2, 2, 4, 2, 16, 128), BF),
    pltpu.VMEM((2, 15, 2, 16, 128), BF),
    pltpu.VMEM((2, 2, 16, 128), BF),
    pltpu.VMEM((7, 16, 128), BF),
    pltpu.SemaphoreType.DMA((2, 39)),
]
ROWS = pltpu.VMEM((TOK, D), BF)
WIDE = pltpu.VMEM((TOK, D), F32)
SQUARE = pltpu.VMEM((D, D), BF)
RAW = pltpu.VMEM((6, 12, 4, D), BF)
PIECES = [pltpu.VMEM((2, 128, D), BF), pltpu.VMEM((2, 64, 256), BF)]
TAILS = pltpu.VMEM((2, 4, 16, 256), BF)
SEMS = pltpu.SemaphoreType.DMA((2, 4, 2))


def whole(
    sizes, factor, tok_in, cot_in, scale_in, wq_in, wk_in, wv_in, wo_in, down_in, up_in, pack_in, ends_in,
    main_back, tail_back, down_out, up_out,
    raw_tok, raw_cot, scale, wq, wk, wv, wo, acat, ups, pack_table, ends, load, wide,
    main_tok, tail_tok, main_cot, tail_cot, tails_tok, tails_cot, tails_out,
    send_tok, recv_tok, send_cot, recv_cot, send_out, recv_out,
    w_tok, w_cot, hs, q, k, v, da, at, dq, dk, dv, dh, tg, low, back, mean, rstd, bias,
    gt, r1, s1, r2, s2, r3, sems,
):
    reducer = Reducer()
    partners = ring_of(sizes) + reducer.partners()
    moves = [
        (tok_in, raw_tok), (pack_in, pack_table), (cot_in, raw_cot), (ends_in, ends), (scale_in, scale),
        (down_in, acat), (up_in, ups), (wq_in, wq), (wk_in, wk), (wv_in, wv), (wo_in, wo),
    ]
    loads = [pltpu.make_async_copy(a, b, load.at[n]) for n, (a, b) in enumerate(moves)]
    for copy in loads[:3]:
        copy.start()
    start_barrier(partners)
    weights = (wq, wk, wv, wo)

    loads[0].wait()
    for copy in loads[3:]:
        copy.start()
    natural_rows(raw_tok, wide)
    loads[1].wait()
    pack(wide, pack_table, main_tok, tail_tok)
    end_barrier(partners)
    tok_copies = in_copies(sizes, main_tok, tail_tok, w_tok, tails_tok, send_tok, recv_tok)
    for copy in tok_copies:
        copy.start()
    keep_own(main_tok, tail_tok, w_tok, tails_tok)
    loads[2].wait()
    natural_rows(raw_cot, wide)
    pack(wide, pack_table, main_cot, tail_cot)
    keep_own(main_cot, tail_cot, w_cot, tails_cot)
    make_bias(sizes, bias)
    for copy in tok_copies:
        copy.wait_send()
    cot_copies = in_copies(sizes, main_cot, tail_cot, w_cot, tails_cot, send_cot, recv_cot)
    for copy in cot_copies:
        copy.start()
    for copy in loads[3:]:
        copy.wait()
    for copy in tok_copies:
        copy.wait_recv()
    for w in range(2):
        tails_to_window(ends, tails_tok[w], w_tok, WIN * w)
    norm_rows(w_tok, scale, hs, mean, rstd)
    project_tokens(hs, weights, ups, acat, low, q, k, v)
    for copy in cot_copies:
        copy.wait()
    for w in range(2):
        tails_to_window(ends, tails_cot[w], w_cot, WIN * w)
    project_cotangent(w_cot, wo, ups, acat, back, da)
    attend(q, k, v, da, bias, at, dq, dk, dv)
    sides = adapter_sides(w_cot, at, dq, dk, dv, ups, acat, low, back)
    first = []
    for part in range(2):
        lora_partials(part, sides, hs, w_cot, at, dq, dk, dv, gt)
        first.append(reducer.start_first(part, gt, r1, sems))
    second = []
    for part in range(2):
        hidden_gradient((part,), weights, dq, dk, dv, acat, back, dh)
        second.append(reducer.start_second(part, first[part], gt, r1, s1, r2, sems))
    hidden_gradient((2, 3), weights, dq, dk, dv, acat, back, dh)
    norm_gradient(w_tok, w_cot, scale, mean, rstd, dh, tg)
    for w in range(2):
        tails_out[w] = window_to_tails(ends, tg[WIN * w + 128 : WIN * w + 144, :])
    out = out_copies(sizes, tg, tails_out, main_back, tail_back, send_out, recv_out)
    for copy in out:
        copy.start()
    return_own(tg, tails_out, main_back, tail_back)
    for part in range(2):
        reducer.sum_second(part, second[part], s1, r2, s2)
    third = reducer.start_third(s2, r3, sems)
    for copy in out:
        copy.wait()
    reducer.finish(third, s2, r3, down_out, up_out, factor)


def unpack(table, main, tail, down, up, grad_out, down_out, up_out, wide):
    for ah in range(2):
        for k in range(4):
            cols = slice(256 * k, 256 * k + 256)
            wide[:, cols] = dot(table[k], jnp.concatenate([main[ah, :, cols], tail[ah]], 0))
        for a in range(3):
            for o in range(12):
                row = (12 * a + o) * 4
                grad_out[3 * ah + a, o] = wide[row : row + 4, :].astype(BF)
    down_out[...] = down[...]
    up_out[...] = up[...]


def vmem(n):
    return [pl.BlockSpec(memory_space=pltpu.VMEM)] * n


def local(
    sizes, tokens, cotangent, norm_scale_vector, query_matrix, key_matrix, value_matrix, output_matrix,
    adapter_down_maps, adapter_up_maps,
):
    pack_table, unpack_table, ends = move_tables()
    factor = float(TOK * sizes["lon"] * sizes["lat"]) ** (-0.5)
    anywhere = pl.BlockSpec(memory_space=pl.ANY)
    results = (
        jax.ShapeDtypeStruct((6, 12, 4, D), BF),
        jax.ShapeDtypeStruct((16, 32), F32),
        jax.ShapeDtypeStruct((16, 32), F32),
    )
    made = pl.pallas_call(
        functools.partial(whole, sizes, factor),
        out_shape=(
            jax.ShapeDtypeStruct((2, 128, D), BF), jax.ShapeDtypeStruct((2, 64, 256), BF), *results[1:],
        ),
        in_specs=[anywhere] * 11,
        out_specs=tuple(vmem(4)),
        scratch_shapes=[
            RAW, RAW, pltpu.VMEM((8, 128), BF), SQUARE, SQUARE, SQUARE, SQUARE,
            pltpu.VMEM((128, D), BF), pltpu.VMEM((128, D), BF),
            pltpu.VMEM((4, 192, 144), BF), pltpu.VMEM((128, 64), BF), pltpu.SemaphoreType.DMA((11,)), WIDE,
        ]
        + PIECES * 2
        + [TAILS] * 3
        + [SEMS] * 6
        + [ROWS] * 13
        + [
            pltpu.VMEM((TOK, 128), BF), pltpu.VMEM((TOK, 128), BF),
            pltpu.VMEM((TOK, 1), F32), pltpu.VMEM((TOK, 1), F32), pltpu.VMEM((2, WIN, 4 * WIN), F32),
        ]
        + REDUCE_SCRATCH,
        compiler_params=pltpu.CompilerParams(
            collective_id=0, has_side_effects=True, vmem_limit_bytes=VMEM_LIMIT
        ),
    )(
        tokens.transpose(1, 2, 0, 3), cotangent.transpose(1, 2, 0, 3), norm_scale_vector.reshape(8, 128),
        query_matrix, key_matrix, value_matrix, output_matrix,
        adapter_down_maps.transpose(0, 2, 1).reshape(128, D), adapter_up_maps.reshape(128, D),
        pack_table, ends,
    )
    grad, down, up = pl.pallas_call(
        unpack,
        out_shape=results,
        in_specs=vmem(5),
        out_specs=tuple(vmem(3)),
        scratch_shapes=[pltpu.VMEM((WIN, D), F32)],
        compiler_params=pltpu.CompilerParams(vmem_limit_bytes=VMEM_LIMIT),
    )(unpack_table, *made)
    return grad.transpose(2, 0, 1, 3), down, up.T


def solution(mesh):
    sizes = dict(mesh.shape)
    spread = P(None, "lat", "lon", None)
    return jax.shard_map(
        functools.partial(local, sizes),
        mesh=mesh,
        in_specs=(spread, spread, P(), P(), P(), P(), P(), P(), P()),
        out_specs=(spread, P(("lon", "lat"), None), P(None, ("lon", "lat"))),
        check_vma=False,
    )
```

```python
import functools

import jax
import jax.numpy as jnp
import numpy as np
from jax import lax
from jax.experimental import pallas as pl
from jax.experimental.pallas import tpu as pltpu
from jax.sharding import PartitionSpec as P

MESH = pl.DeviceIdType.MESH
BF = jnp.bfloat16
F32 = jnp.float32
EPS = 1e-05
NEG = -1e30
D = 1024
WIN = 144
TOK = 2 * WIN
LEVELS = ((1, 2), (3, 0))
OWN = (3, 0)
VMEM_LIMIT = 60 * 1024 * 1024


def move_tables():
    pack = np.zeros((4, 192, 144), np.float32)
    unpack = np.zeros((4, 144, 192), np.float32)
    ends = np.zeros((128, 64), np.float32)

    def source(w, h, t):
        return (t // 6 % 3) * 48 + (6 * h + t % 6) * 4 + LEVELS[w][t // 18]

    for w in range(2):
        for h in range(2):
            for t in range(32):
                row = 64 * w + 32 * h + t
                pack[:, row, source(w, h, t)] = 1
                unpack[:, source(w, h, t), row] = 1
            for k in range(4):
                for t in range(4):
                    row = 128 + 32 * w + 16 * h + 4 * k + t
                    pack[k, row, source(w, h, 32 + t)] = 1
                    unpack[k, source(w, h, 32 + t), row] = 1
    for p in range(4):
        for k in range(4):
            for t in range(4):
                ends[16 * k + 4 * p + t, 16 * p + 4 * k + t] = 1
                ends[64 + 16 * p + 4 * k + t, 16 * k + 4 * p + t] = 1
    return tuple(jnp.asarray(table, BF) for table in (pack, unpack, ends))


def dot(a, b):
    return jnp.dot(a, b, preferred_element_type=F32)


def dot_nt(a, b):
    return lax.dot_general(a, b, (((1,), (1,)), ((), ())), preferred_element_type=F32)


def dot_tn(a, b):
    return lax.dot_general(a, b, (((0,), (0,)), ((), ())), preferred_element_type=F32)


def neighbour(sizes, lat_step, lon_step):
    lon = lax.rem(lax.axis_index("lon") + lon_step + sizes["lon"], sizes["lon"])
    lat = lax.rem(lax.axis_index("lat") + lat_step + sizes["lat"], sizes["lat"])
    return (lon, lat)


def steps_of(w, p):
    differs = p ^ OWN[w]
    sign = -1 if w == 0 else 1
    return sign * (differs >> 1), sign * (differs & 1)


def moving_pieces():
    return [(w, OWN[w] ^ differs) for differs in (3, 1, 2) for w in range(2)]


def ring_of(sizes):
    return [neighbour(sizes, *steps_of(w, p)) for w, p in moving_pieces()]


def remote(src, dst, send, recv, device):
    return pltpu.make_async_remote_copy(
        src_ref=src, dst_ref=dst, send_sem=send, recv_sem=recv, device_id=device, device_id_type=MESH
    )


def natural_rows(raw, wide):
    for a in range(6):
        for o in range(12):
            row = (12 * a + o) * 4
            wide[row : row + 4, :] = raw[a, o].astype(F32)


def piece_rows(w, p):
    return p >> 1, 64 * w + 32 * (p & 1)


def pack(natural, table, main, tail):
    for ah in range(2):
        rows = natural[WIN * ah : WIN * ah + WIN, :].astype(BF)
        ends = jnp.zeros((64, 256), F32)
        for k in range(4):
            cols = slice(256 * k, 256 * k + 256)
            moved = dot(table[k], rows[:, cols])
            main[ah, :, cols] = moved[0:128].astype(BF)
            ends = ends + moved[128:192]
        tail[ah] = ends.astype(BF)


def tails_to_window(table, tails, window, first):
    stacked = tails.reshape(64, 256)
    for k in range(4):
        window[first + 128 : first + 144, 256 * k : 256 * k + 256] = dot(
            table[16 * k : 16 * k + 16, :], stacked
        ).astype(BF)


def window_to_tails(table, rows):
    ends = jnp.zeros((64, 256), F32)
    for k in range(4):
        ends = ends + dot(
            table[64:128, 16 * k : 16 * k + 16], rows[:, 256 * k : 256 * k + 256]
        )
    return ends.astype(BF).reshape(4, 16, 256)


def in_copies(sizes, main, tail, window, tails, send, recv):
    copies = []
    for w, p in moving_pieces():
        device = neighbour(sizes, *steps_of(w, p))
        ah, row = piece_rows(w, p)
        copies.append(
            remote(
                main.at[ah, pl.ds(row, 32)], window.at[pl.ds(WIN * w + 32 * p, 32)],
                send.at[w, p, 0], recv.at[w, p, 0], device,
            )
        )
        copies.append(
            remote(
                tail.at[ah, pl.ds(row // 2, 16)], tails.at[w, p],
                send.at[w, p, 1], recv.at[w, p, 1], device,
            )
        )
    return copies


def keep_own(main, tail, window, tails):
    for w in range(2):
        p = OWN[w]
        ah, row = piece_rows(w, p)
        window[WIN * w + 32 * p : WIN * w + 32 * p + 32, :] = main[ah, row : row + 32]
        tails[w, p] = tail[ah, row // 2 : row // 2 + 16]


def out_copies(window, sizes, tg, tg_tail, main, tail, send, recv):
    copies = []
    for w, p in moving_pieces():
        if w != window:
            continue
        lat_step, lon_step = steps_of(w, p)
        device = neighbour(sizes, -lat_step, -lon_step)
        ah, row = piece_rows(w, p)
        copies.append(
            remote(
                tg.at[pl.ds(32 * p, 32)], main.at[ah, pl.ds(row, 32)],
                send.at[w, p, 0], recv.at[w, p, 0], device,
            )
        )
        copies.append(
            remote(
                tg_tail.at[w, p], tail.at[ah, pl.ds(row // 2, 16)],
                send.at[w, p, 1], recv.at[w, p, 1], device,
            )
        )
    return copies


def return_own(tgs, tg_tail, main, tail):
    for w in range(2):
        p = OWN[w]
        ah, row = piece_rows(w, p)
        main[ah, row : row + 32] = tgs[w][32 * p : 32 * p + 32, :]
        tail[ah, row // 2 : row // 2 + 16] = tg_tail[w, p]


def start_barrier(devices):
    barrier = pltpu.get_barrier_semaphore()
    for device in devices:
        pl.semaphore_signal(barrier, inc=1, device_id=device, device_id_type=MESH)


def end_barrier(devices):
    pl.semaphore_wait(pltpu.get_barrier_semaphore(), len(devices))


def gain_of(scale):
    rows = scale[...].astype(F32)
    return jnp.concatenate([rows[n : n + 1] for n in range(8)], 1)


def slot_lanes(values, slots):
    lane = lax.broadcasted_iota(jnp.int32, values.shape, 1) // 32
    keep = lane == slots[0]
    for slot in slots[1:]:
        keep = keep | (lane == slot)
    return jnp.where(keep, values, 0.0)


def norm_rows(w_tok, scale, hs, mean, rstd):
    gain = gain_of(scale)

    def body(i, carry):
        rows = pl.ds(pl.multiple_of(i * 48, 48), 48)
        x = w_tok[rows, :].astype(F32)
        mu = jnp.mean(x, axis=-1, keepdims=True)
        center = x - mu
        inverse = lax.rsqrt(jnp.mean(center * center, axis=-1, keepdims=True) + EPS)
        mean[rows, :] = mu
        rstd[rows, :] = inverse
        hs[rows, :] = (center * inverse * gain).astype(BF)
        return carry

    lax.fori_loop(0, TOK // 48, body, 0, unroll=2)


def project_tokens(hs, weights, ups, acat, low, q, k, v):
    low[...] = dot_nt(hs[...], acat[...]).astype(BF)
    lows = [slot_lanes(low[...].astype(F32), (n,)).astype(BF) for n in range(3)]
    for c in range(4):
        cols = slice(256 * c, 256 * c + 256)
        for n, (w, out) in enumerate(zip(weights[:3], (q, k, v))):
            out[:, cols] = (dot(hs[...], w[:, cols]) + dot(lows[n], ups[:, cols])).astype(BF)


def project_cotangent(w_cot, wo, ups, acat, back, da):
    back[...] = slot_lanes(dot_nt(w_cot[...], ups[...]), (3,)).astype(BF)
    for c in range(4):
        cols = slice(256 * c, 256 * c + 256)
        da[:, cols] = (dot_nt(w_cot[...], wo[cols, :]) + dot(back[...], acat[:, cols])).astype(BF)


def make_bias(sizes, bias):
    lat = lax.axis_index("lat")

    def coordinates(r):
        tail = r >= 128
        piece = jnp.where(tail, (r - 128) // 4, r // 32)
        t = jnp.where(tail, 32 + r % 4, r % 32)
        return (piece < 2).astype(jnp.int32), (t >= 18).astype(jnp.int32)

    key_ah, key_lv = coordinates(lax.broadcasted_iota(jnp.int32, (WIN, 4 * WIN), 0))
    c = lax.broadcasted_iota(jnp.int32, (WIN, 4 * WIN), 1)
    for n in (3, 2, 1):
        c = jnp.where(c >= n * WIN, c - n * WIN, c)
    query_ah, query_lv = coordinates(c)
    for w in range(2):
        last = (lat == (sizes["lat"] - 1 if w == 0 else 0)).astype(jnp.int32)
        differs = (key_ah != query_ah).astype(jnp.int32) * last
        if w == 1:
            differs = differs + (key_lv != query_lv).astype(jnp.int32)
        bias[w] = jnp.where(differs > 0, NEG, 0.0).astype(F32)


def attend(q, k, v, da, bias, at, dq, dk, dv):
    lane = lax.broadcasted_iota(jnp.int32, (1, 256), 1) // 64
    masks = [(lane == h).astype(F32).astype(BF) for h in range(4)]
    lanes = lax.broadcasted_iota(jnp.int32, (WIN, 256), 1) // 64

    def stacked(values):
        return jnp.concatenate([values * mask for mask in masks], 0)

    def own_blocks(values):
        result = values[0:WIN]
        for h in range(1, 4):
            result = jnp.where(lanes == h, values[WIN * h : WIN * h + WIN], result)
        return result

    def body(c, carry):
        cols = pl.ds(pl.multiple_of(c * 256, 256), 256)
        for w in range(2):
            rows = pl.ds(WIN * w, WIN)
            kk = k[rows, cols]
            vv = v[rows, cols]
            q4 = stacked(q[rows, cols] * jnp.asarray(0.125, BF))
            d4 = stacked(da[rows, cols])
            s = dot_nt(kk, q4) + bias[w]
            e = jnp.exp(s - jnp.max(s, axis=0, keepdims=True))
            p = e * (1.0 / jnp.sum(e, axis=0, keepdims=True))
            dp = dot_nt(vv, d4)
            ds = (p * (dp - jnp.sum(dp * p, axis=0, keepdims=True))).astype(BF)
            pb = p.astype(BF)
            dv[rows, cols] = dot(pb, d4).astype(BF)
            dk[rows, cols] = dot(ds, q4).astype(BF)
            at[rows, cols] = own_blocks(dot_tn(pb, vv)).astype(BF)
            dq[rows, cols] = (own_blocks(dot_tn(ds, kk)) * 0.125).astype(BF)
        return carry

    lax.fori_loop(0, 4, body, 0, unroll=2)


def adapter_sides(w_cot, at, dq, dk, dv, ups, acat, low, back):
    lane = lax.broadcasted_iota(jnp.int32, (TOK, 128), 1) // 32
    backs = back[...].astype(F32)
    for n, d in enumerate((dq, dk, dv)):
        backs = jnp.where(lane == n, dot_nt(d[...], ups[...]), backs)
    back[...] = backs.astype(BF)
    lows = jnp.where(lane == 3, dot_nt(at[...], acat[...]), low[...].astype(F32))
    return backs.T.astype(BF), lows.T.astype(BF)


def lora_partials(z1, sides, hs, w_cot, at, dq, dk, dv, gt):
    back_t, low_t = sides
    for z0 in range(2):
        c = 2 * z1 + z0
        cols = slice(256 * c, 256 * c + 256)
        own_down = dot(back_t[0:96], hs[:, cols])
        last_down = dot(back_t[96:128], at[:, cols])
        ups_own = [dot(low_t[32 * n : 32 * n + 32], d[:, cols]) for n, d in enumerate((dq, dk, dv, w_cot))]
        parts = []
        for n in range(4):
            parts.append(own_down[32 * n : 32 * n + 32] if n < 3 else last_down)
            parts.append(ups_own[n])
        block = jnp.concatenate(parts, 0)
        for half in range(2):
            turned = block[:, 128 * half : 128 * half + 128].T.astype(BF)
            for b in range(8):
                y, lat = 2 * half + b // 4, b % 4
                rows = turned[16 * b : 16 * b + 16]
                for xh in range(2):
                    gt[lat % 2, z1, xh, lat // 2, y, z0] = rows[:, 128 * xh : 128 * xh + 128]


def hidden_gradient(w, chunks, weights, dq, dk, dv, acat, back, dh):
    rows = slice(WIN * w, WIN * w + WIN)
    backs = slot_lanes(back[rows, :].astype(F32), (0, 1, 2)).astype(BF)
    for c in chunks:
        cols = slice(256 * c, 256 * c + 256)
        total = dot(backs, acat[:, cols])
        for weight, d in zip(weights[:3], (dq, dk, dv)):
            total = total + dot_nt(d[rows, :], weight[cols, :])
        dh[rows, cols] = total.astype(BF)


def norm_gradient(w, w_tok, w_cot, scale, mean, rstd, dh, tg):
    gain = gain_of(scale)
    for i in range(0, WIN, 48):
        rows = slice(WIN * w + i, WIN * w + i + 48)
        inverse = rstd[rows, :]
        xhat = (w_tok[rows, :].astype(F32) - mean[rows, :]) * inverse
        g = dh[rows, :].astype(F32) * gain
        first = jnp.mean(g, axis=-1, keepdims=True)
        second = jnp.mean(g * xhat, axis=-1, keepdims=True)
        tg[i : i + 48, :] = (w_cot[rows, :].astype(F32) + inverse * (g - first - xhat * second)).astype(BF)


class Reducer:
    def __init__(self):
        lon = lax.axis_index("lon")
        lat = lax.axis_index("lat")
        y = lax.rem(lon, 4)
        z = lax.rem(lon // 4, 8)
        xh, xl, core = lon // 32, lat // 2, lax.rem(lat, 2)
        self.core, self.z = core, z
        self.mine = (xh, xl, y)

        def device(xh, z, y, xl, core):
            return ((xh * 8 + z) * 4 + y, xl * 2 + core)

        self.first = device(xh, z, y, xl, 1 - core)
        self.second = []
        for n in (10, 2, 6, 14, 9, 11, 8, 1, 3, 5, 7, 13, 15, 4, 12):
            to = lax.rem(xh + n // 8, 2), lax.rem(xl + n // 4, 2), lax.rem(y + n, 4)
            self.second.append((n - 1, to, device(to[0], z, to[2], to[1], core)))
        self.third = []
        for n in (4, 3, 5, 2, 6, 1, 7):
            to = lax.rem(z + n, 8)
            self.third.append((n - 1, to, device(xh, to, y, xl, core)))

    def partners(self):
        return [self.first] + [s[-1] for s in self.second] + [s[-1] for s in self.third]

    def start_first(self, part, gt, r1, sems):
        copy = remote(gt.at[1 - self.core, part], r1.at[part], sems.at[0, part], sems.at[1, part], self.first)
        copy.start()
        return copy

    def start_second(self, part, copy, gt, r1, s1, r2, sems):
        copy.wait()
        s1[part] = (gt[self.core, part].astype(F32) + r1[part].astype(F32)).astype(BF)
        copies = []
        for n, to, device in self.second:
            sem = 2 + 15 * part + n
            copies.append(
                remote(s1.at[part, to[0], to[1], to[2]], r2.at[part, n], sems.at[0, sem], sems.at[1, sem], device)
            )
            copies[-1].start()
        return copies

    def sum_second(self, part, copies, s1, r2, s2):
        total = s1[part, self.mine[0], self.mine[1], self.mine[2]].astype(F32)
        for copy in copies:
            copy.wait()
        for n in range(15):
            total = total + r2[part, n].astype(F32)
        s2[part] = total.astype(BF)

    def start_third(self, s2, r3, sems):
        copies = []
        for n, to, device in self.third:
            sem = 32 + n
            block = s2.at[lax.rem(to // 2, 2), lax.rem(to, 2)]
            copies.append(remote(block, r3.at[n], sems.at[0, sem], sems.at[1, sem], device))
            copies[-1].start()
        return copies

    def finish(self, copies, s2, r3, down_out, up_out, factor):
        total = s2[lax.rem(self.z // 2, 2), lax.rem(self.z, 2)].astype(F32)
        for copy in copies:
            copy.wait()
        for n in range(7):
            total = total + r3[n].astype(F32)
        total = total * factor
        total = jnp.where(self.z < 4, total[:, 0:64], total[:, 64:128])
        down_out[...] = total[:, 0:32]
        up_out[...] = total[:, 32:64]


REDUCE_SCRATCH = [
    pltpu.VMEM((2, 2, 2, 2, 4, 2, 16, 128), BF),
    pltpu.VMEM((2, 2, 2, 4, 2, 16, 128), BF),
    pltpu.VMEM((2, 2, 2, 4, 2, 16, 128), BF),
    pltpu.VMEM((2, 15, 2, 16, 128), BF),
    pltpu.VMEM((2, 2, 16, 128), BF),
    pltpu.VMEM((7, 16, 128), BF),
    pltpu.SemaphoreType.DMA((2, 39)),
]
ROWS = pltpu.VMEM((TOK, D), BF)
WIDE = pltpu.VMEM((TOK, D), F32)
SQUARE = pltpu.VMEM((D, D), BF)
RAW = pltpu.VMEM((6, 12, 4, D), BF)
PIECES = [pltpu.VMEM((2, 128, D), BF), pltpu.VMEM((2, 64, 256), BF)]
TAILS = pltpu.VMEM((2, 4, 16, 256), BF)
SEMS = pltpu.SemaphoreType.DMA((2, 4, 2))


def whole(
    sizes, factor, tok_in, cot_in, scale_in, wq_in, wk_in, wv_in, wo_in, down_in, up_in, pack_in, ends_in,
    main_back, tail_back, down_out, up_out,
    raw_tok, raw_cot, scale, wq, wk, wv, wo, acat, ups, pack_table, ends, load, wide,
    main_tok, tail_tok, main_cot, tail_cot, tails_tok, tails_cot, tails_out,
    send_tok, recv_tok, send_cot, recv_cot, send_out, recv_out,
    w_tok, w_cot, hs, q, k, v, da, at, dq, dk, dv, dh, tg_a, tg_b, low, back, mean, rstd, bias,
    gt, r1, s1, r2, s2, r3, sems,
):
    reducer = Reducer()
    partners = ring_of(sizes) + reducer.partners()
    moves = [
        (tok_in, raw_tok), (pack_in, pack_table), (cot_in, raw_cot), (ends_in, ends), (scale_in, scale),
        (down_in, acat), (up_in, ups), (wq_in, wq), (wk_in, wk), (wv_in, wv), (wo_in, wo),
    ]
    loads = [pltpu.make_async_copy(a, b, load.at[n]) for n, (a, b) in enumerate(moves)]
    for copy in loads[:3]:
        copy.start()
    start_barrier(partners)
    weights = (wq, wk, wv, wo)

    loads[0].wait()
    for copy in loads[3:]:
        copy.start()
    natural_rows(raw_tok, wide)
    loads[1].wait()
    pack(wide, pack_table, main_tok, tail_tok)
    end_barrier(partners)
    tok_copies = in_copies(sizes, main_tok, tail_tok, w_tok, tails_tok, send_tok, recv_tok)
    for copy in tok_copies:
        copy.start()
    keep_own(main_tok, tail_tok, w_tok, tails_tok)
    loads[2].wait()
    natural_rows(raw_cot, wide)
    pack(wide, pack_table, main_cot, tail_cot)
    keep_own(main_cot, tail_cot, w_cot, tails_cot)
    make_bias(sizes, bias)
    cot_copies = in_copies(sizes, main_cot, tail_cot, w_cot, tails_cot, send_cot, recv_cot)
    for ahead, copy in reversed(list(zip(tok_copies, cot_copies))):
        ahead.wait_send()
        copy.start()
    for copy in loads[3:]:
        copy.wait()
    for copy in tok_copies:
        copy.wait_recv()
    for w in range(2):
        tails_to_window(ends, tails_tok[w], w_tok, WIN * w)
    norm_rows(w_tok, scale, hs, mean, rstd)
    project_tokens(hs, weights, ups, acat, low, q, k, v)
    for copy in cot_copies:
        copy.wait()
    for w in range(2):
        tails_to_window(ends, tails_cot[w], w_cot, WIN * w)
    project_cotangent(w_cot, wo, ups, acat, back, da)
    attend(q, k, v, da, bias, at, dq, dk, dv)
    sides = adapter_sides(w_cot, at, dq, dk, dv, ups, acat, low, back)
    first = []
    for part in range(2):
        lora_partials(part, sides, hs, w_cot, at, dq, dk, dv, gt)
        first.append(reducer.start_first(part, gt, r1, sems))
    second = []
    out = []
    for w, tg in enumerate((tg_a, tg_b)):
        for part in range(2):
            hidden_gradient(w, (2 * part, 2 * part + 1), weights, dq, dk, dv, acat, back, dh)
            if w == 0:
                second.append(reducer.start_second(part, first[part], gt, r1, s1, r2, sems))
        norm_gradient(w, w_tok, w_cot, scale, mean, rstd, dh, tg)
        tails_out[w] = window_to_tails(ends, tg[128:144, :])
        for copy in out_copies(w, sizes, tg, tails_out, main_back, tail_back, send_out, recv_out):
            copy.start()
            out.append(copy)
    return_own((tg_a, tg_b), tails_out, main_back, tail_back)
    for part in range(2):
        reducer.sum_second(part, second[part], s1, r2, s2)
    third = reducer.start_third(s2, r3, sems)
    for copy in out:
        copy.wait()
    reducer.finish(third, s2, r3, down_out, up_out, factor)


def unpack(table, main, tail, down, up, grad_out, down_out, up_out, wide):
    for ah in range(2):
        for k in range(4):
            cols = slice(256 * k, 256 * k + 256)
            wide[:, cols] = dot(table[k], jnp.concatenate([main[ah, :, cols], tail[ah]], 0))
        for a in range(3):
            for o in range(12):
                row = (12 * a + o) * 4
                grad_out[3 * ah + a, o] = wide[row : row + 4, :].astype(BF)
    down_out[...] = down[...]
    up_out[...] = up[...]


def vmem(n):
    return [pl.BlockSpec(memory_space=pltpu.VMEM)] * n


def local(
    sizes, tokens, cotangent, norm_scale_vector, query_matrix, key_matrix, value_matrix, output_matrix,
    adapter_down_maps, adapter_up_maps,
):
    pack_table, unpack_table, ends = move_tables()
    factor = float(TOK * sizes["lon"] * sizes["lat"]) ** (-0.5)
    anywhere = pl.BlockSpec(memory_space=pl.ANY)
    results = (
        jax.ShapeDtypeStruct((6, 12, 4, D), BF),
        jax.ShapeDtypeStruct((16, 32), F32),
        jax.ShapeDtypeStruct((16, 32), F32),
    )
    made = pl.pallas_call(
        functools.partial(whole, sizes, factor),
        out_shape=(
            jax.ShapeDtypeStruct((2, 128, D), BF), jax.ShapeDtypeStruct((2, 64, 256), BF), *results[1:],
        ),
        in_specs=[anywhere] * 11,
        out_specs=tuple(vmem(4)),
        scratch_shapes=[
            RAW, RAW, pltpu.VMEM((8, 128), BF), SQUARE, SQUARE, SQUARE, SQUARE,
            pltpu.VMEM((128, D), BF), pltpu.VMEM((128, D), BF),
            pltpu.VMEM((4, 192, 144), BF), pltpu.VMEM((128, 64), BF), pltpu.SemaphoreType.DMA((11,)), WIDE,
        ]
        + PIECES * 2
        + [TAILS] * 3
        + [SEMS] * 6
        + [ROWS] * 12
        + [pltpu.VMEM((WIN, D), BF)] * 2
        + [
            pltpu.VMEM((TOK, 128), BF), pltpu.VMEM((TOK, 128), BF),
            pltpu.VMEM((TOK, 1), F32), pltpu.VMEM((TOK, 1), F32), pltpu.VMEM((2, WIN, 4 * WIN), F32),
        ]
        + REDUCE_SCRATCH,
        compiler_params=pltpu.CompilerParams(
            collective_id=0, has_side_effects=True, vmem_limit_bytes=VMEM_LIMIT
        ),
    )(
        tokens.transpose(1, 2, 0, 3), cotangent.transpose(1, 2, 0, 3), norm_scale_vector.reshape(8, 128),
        query_matrix, key_matrix, value_matrix, output_matrix,
        adapter_down_maps.transpose(0, 2, 1).reshape(128, D), adapter_up_maps.reshape(128, D),
        pack_table, ends,
    )
    grad, down, up = pl.pallas_call(
        unpack,
        out_shape=results,
        in_specs=vmem(5),
        out_specs=tuple(vmem(3)),
        scratch_shapes=[pltpu.VMEM((WIN, D), F32)],
        compiler_params=pltpu.CompilerParams(vmem_limit_bytes=VMEM_LIMIT),
    )(unpack_table, *made)
    return grad.transpose(2, 0, 1, 3), down, up.T


def solution(mesh):
    sizes = dict(mesh.shape)
    spread = P(None, "lat", "lon", None)
    return jax.shard_map(
        functools.partial(local, sizes),
        mesh=mesh,
        in_specs=(spread, spread, P(), P(), P(), P(), P(), P(), P()),
        out_specs=(spread, P(("lon", "lat"), None), P(None, ("lon", "lat"))),
        check_vma=False,
    )
```

```python
import functools

import jax
import jax.numpy as jnp
import numpy as np
from jax import lax
from jax.experimental import pallas as pl
from jax.experimental.pallas import tpu as pltpu
from jax.sharding import PartitionSpec as P

MESH = pl.DeviceIdType.MESH
BF = jnp.bfloat16
F32 = jnp.float32
EPS = 1e-05
NEG = -1e30
D = 1024
WIN = 144
TOK = 2 * WIN
LEVELS = ((1, 2), (3, 0))
OWN = (3, 0)
VMEM_LIMIT = 60 * 1024 * 1024


def move_tables():
    pack = np.zeros((4, 192, 144), np.float32)
    unpack = np.zeros((4, 144, 192), np.float32)
    ends = np.zeros((128, 64), np.float32)

    def source(w, h, t):
        return (t // 6 % 3) * 48 + (6 * h + t % 6) * 4 + LEVELS[w][t // 18]

    for w in range(2):
        for h in range(2):
            for t in range(32):
                row = 64 * w + 32 * h + t
                pack[:, row, source(w, h, t)] = 1
                unpack[:, source(w, h, t), row] = 1
            for k in range(4):
                for t in range(4):
                    row = 128 + 32 * w + 16 * h + 4 * k + t
                    pack[k, row, source(w, h, 32 + t)] = 1
                    unpack[k, source(w, h, 32 + t), row] = 1
    for p in range(4):
        for k in range(4):
            for t in range(4):
                ends[16 * k + 4 * p + t, 16 * p + 4 * k + t] = 1
                ends[64 + 16 * p + 4 * k + t, 16 * k + 4 * p + t] = 1
    return tuple(jnp.asarray(table, BF) for table in (pack, unpack, ends))


def dot(a, b):
    return jnp.dot(a, b, preferred_element_type=F32)


def dot_nt(a, b):
    return lax.dot_general(a, b, (((1,), (1,)), ((), ())), preferred_element_type=F32)


def dot_tn(a, b):
    return lax.dot_general(a, b, (((0,), (0,)), ((), ())), preferred_element_type=F32)


def neighbour(sizes, lat_step, lon_step):
    lon = lax.rem(lax.axis_index("lon") + lon_step + sizes["lon"], sizes["lon"])
    lat = lax.rem(lax.axis_index("lat") + lat_step + sizes["lat"], sizes["lat"])
    return (lon, lat)


def steps_of(w, p):
    differs = p ^ OWN[w]
    sign = -1 if w == 0 else 1
    return sign * (differs >> 1), sign * (differs & 1)


def moving_pieces():
    return [(w, OWN[w] ^ differs) for differs in (3, 1, 2) for w in range(2)]


def ring_of(sizes):
    return [neighbour(sizes, *steps_of(w, p)) for w, p in moving_pieces()]


def remote(src, dst, send, recv, device):
    return pltpu.make_async_remote_copy(
        src_ref=src, dst_ref=dst, send_sem=send, recv_sem=recv, device_id=device, device_id_type=MESH
    )


def natural_rows(raw, wide):
    for a in range(6):
        for o in range(12):
            row = (12 * a + o) * 4
            wide[row : row + 4, :] = raw[a, o].astype(F32)


def piece_rows(w, p):
    return p >> 1, 64 * w + 32 * (p & 1)


def pack(natural, table, main, tail):
    for ah in range(2):
        rows = natural[WIN * ah : WIN * ah + WIN, :].astype(BF)
        ends = jnp.zeros((64, 256), F32)
        for k in range(4):
            cols = slice(256 * k, 256 * k + 256)
            moved = dot(table[k], rows[:, cols])
            main[ah, :, cols] = moved[0:128].astype(BF)
            ends = ends + moved[128:192]
        tail[ah] = ends.astype(BF)


def tails_to_window(table, tails, window, first):
    stacked = tails.reshape(64, 256)
    for k in range(4):
        window[first + 128 : first + 144, 256 * k : 256 * k + 256] = dot(
            table[16 * k : 16 * k + 16, :], stacked
        ).astype(BF)


def window_to_tails(table, rows):
    ends = jnp.zeros((64, 256), F32)
    for k in range(4):
        ends = ends + dot(
            table[64:128, 16 * k : 16 * k + 16], rows[:, 256 * k : 256 * k + 256]
        )
    return ends.astype(BF).reshape(4, 16, 256)


def in_copies(sizes, main, tail, window, tails, send, recv):
    copies = []
    for w, p in moving_pieces():
        device = neighbour(sizes, *steps_of(w, p))
        ah, row = piece_rows(w, p)
        copies.append(
            remote(
                main.at[ah, pl.ds(row, 32)], window.at[pl.ds(WIN * w + 32 * p, 32)],
                send.at[w, p, 0], recv.at[w, p, 0], device,
            )
        )
        copies.append(
            remote(
                tail.at[ah, pl.ds(row // 2, 16)], tails.at[w, p],
                send.at[w, p, 1], recv.at[w, p, 1], device,
            )
        )
    return copies


def keep_own(main, tail, window, tails):
    for w in range(2):
        p = OWN[w]
        ah, row = piece_rows(w, p)
        window[WIN * w + 32 * p : WIN * w + 32 * p + 32, :] = main[ah, row : row + 32]
        tails[w, p] = tail[ah, row // 2 : row // 2 + 16]


def out_copies(window, sizes, tg, tg_tail, main, tail, send, recv):
    copies = []
    for w, p in moving_pieces():
        if w != window:
            continue
        lat_step, lon_step = steps_of(w, p)
        device = neighbour(sizes, -lat_step, -lon_step)
        ah, row = piece_rows(w, p)
        copies.append(
            remote(
                tg.at[pl.ds(32 * p, 32)], main.at[ah, pl.ds(row, 32)],
                send.at[w, p, 0], recv.at[w, p, 0], device,
            )
        )
        copies.append(
            remote(
                tg_tail.at[w, p], tail.at[ah, pl.ds(row // 2, 16)],
                send.at[w, p, 1], recv.at[w, p, 1], device,
            )
        )
    return copies


def return_own(tgs, tg_tail, main, tail):
    for w in range(2):
        p = OWN[w]
        ah, row = piece_rows(w, p)
        main[ah, row : row + 32] = tgs[w][32 * p : 32 * p + 32, :]
        tail[ah, row // 2 : row // 2 + 16] = tg_tail[w, p]


def start_barrier(devices):
    barrier = pltpu.get_barrier_semaphore()
    for device in devices:
        pl.semaphore_signal(barrier, inc=1, device_id=device, device_id_type=MESH)


def end_barrier(devices):
    pl.semaphore_wait(pltpu.get_barrier_semaphore(), len(devices))


def gain_of(scale):
    rows = scale[...].astype(F32)
    return jnp.concatenate([rows[n : n + 1] for n in range(8)], 1)


def slot_lanes(values, slots):
    lane = lax.broadcasted_iota(jnp.int32, values.shape, 1) // 32
    keep = lane == slots[0]
    for slot in slots[1:]:
        keep = keep | (lane == slot)
    return jnp.where(keep, values, 0.0)


def norm_rows(w_tok, scale, hs, mean, rstd):
    gain = gain_of(scale)

    def body(i, carry):
        rows = pl.ds(pl.multiple_of(i * 48, 48), 48)
        x = w_tok[rows, :].astype(F32)
        mu = jnp.mean(x, axis=-1, keepdims=True)
        center = x - mu
        inverse = lax.rsqrt(jnp.mean(center * center, axis=-1, keepdims=True) + EPS)
        mean[rows, :] = mu
        rstd[rows, :] = inverse
        hs[rows, :] = (center * inverse * gain).astype(BF)
        return carry

    lax.fori_loop(0, TOK // 48, body, 0, unroll=2)


def project_tokens(hs, weights, ups, acat, low, q, k, v):
    low[...] = dot_nt(hs[...], acat[...]).astype(BF)
    lows = [slot_lanes(low[...].astype(F32), (n,)).astype(BF) for n in range(3)]
    for c in range(4):
        cols = slice(256 * c, 256 * c + 256)
        for n, (w, out) in enumerate(zip(weights[:3], (q, k, v))):
            out[:, cols] = (dot(hs[...], w[:, cols]) + dot(lows[n], ups[:, cols])).astype(BF)


def project_cotangent(w_cot, wo, ups, acat, back, da):
    back[...] = slot_lanes(dot_nt(w_cot[...], ups[...]), (3,)).astype(BF)
    for c in range(4):
        cols = slice(256 * c, 256 * c + 256)
        da[:, cols] = (dot_nt(w_cot[...], wo[cols, :]) + dot(back[...], acat[:, cols])).astype(BF)


def make_bias(sizes, bias):
    lat = lax.axis_index("lat")

    def coordinates(r):
        tail = r >= 128
        piece = jnp.where(tail, (r - 128) // 4, r // 32)
        t = jnp.where(tail, 32 + r % 4, r % 32)
        return (piece < 2).astype(jnp.int32), (t >= 18).astype(jnp.int32)

    key_ah, key_lv = coordinates(lax.broadcasted_iota(jnp.int32, (WIN, 4 * WIN), 0))
    c = lax.broadcasted_iota(jnp.int32, (WIN, 4 * WIN), 1)
    for n in (3, 2, 1):
        c = jnp.where(c >= n * WIN, c - n * WIN, c)
    query_ah, query_lv = coordinates(c)
    for w in range(2):
        last = (lat == (sizes["lat"] - 1 if w == 0 else 0)).astype(jnp.int32)
        differs = (key_ah != query_ah).astype(jnp.int32) * last
        if w == 1:
            differs = differs + (key_lv != query_lv).astype(jnp.int32)
        bias[w] = jnp.where(differs > 0, NEG, 0.0).astype(F32)


def attend(q, k, v, da, bias, at, dq, dk, dv):
    lane = lax.broadcasted_iota(jnp.int32, (1, 256), 1) // 64
    masks = [(lane == h).astype(F32).astype(BF) for h in range(4)]
    lanes = lax.broadcasted_iota(jnp.int32, (WIN, 256), 1) // 64

    def stacked(values):
        return jnp.concatenate([values * mask for mask in masks], 0)

    def own_blocks(values):
        result = values[0:WIN]
        for h in range(1, 4):
            result = jnp.where(lanes == h, values[WIN * h : WIN * h + WIN], result)
        return result

    def body(c, carry):
        cols = pl.ds(pl.multiple_of(c * 256, 256), 256)
        for w in range(2):
            rows = pl.ds(WIN * w, WIN)
            kk = k[rows, cols]
            vv = v[rows, cols]
            q4 = stacked(q[rows, cols] * jnp.asarray(0.125, BF))
            d4 = stacked(da[rows, cols])
            s = dot_nt(kk, q4) + bias[w]
            e = jnp.exp(s - jnp.max(s, axis=0, keepdims=True))
            p = e * (1.0 / jnp.sum(e, axis=0, keepdims=True))
            dp = dot_nt(vv, d4)
            ds = (p * (dp - jnp.sum(dp * p, axis=0, keepdims=True))).astype(BF)
            pb = p.astype(BF)
            dv[rows, cols] = dot(pb, d4).astype(BF)
            dk[rows, cols] = dot(ds, q4).astype(BF)
            at[rows, cols] = own_blocks(dot_tn(pb, vv)).astype(BF)
            dq[rows, cols] = (own_blocks(dot_tn(ds, kk)) * 0.125).astype(BF)
        return carry

    lax.fori_loop(0, 4, body, 0, unroll=2)


def adapter_sides(w_cot, at, dq, dk, dv, ups, acat, low, back):
    lane = lax.broadcasted_iota(jnp.int32, (TOK, 128), 1) // 32
    backs = back[...].astype(F32)
    for n, d in enumerate((dq, dk, dv)):
        backs = jnp.where(lane == n, dot_nt(d[...], ups[...]), backs)
    back[...] = backs.astype(BF)
    lows = jnp.where(lane == 3, dot_nt(at[...], acat[...]), low[...].astype(F32))
    return backs.T.astype(BF), lows.T.astype(BF)


def lora_partials(z1, sides, hs, w_cot, at, dq, dk, dv, gt):
    back_t, low_t = sides
    for z0 in range(2):
        c = 2 * z1 + z0
        cols = slice(256 * c, 256 * c + 256)
        own_down = dot(back_t[0:96], hs[:, cols])
        last_down = dot(back_t[96:128], at[:, cols])
        ups_own = [dot(low_t[32 * n : 32 * n + 32], d[:, cols]) for n, d in enumerate((dq, dk, dv, w_cot))]
        parts = []
        for n in range(4):
            parts.append(own_down[32 * n : 32 * n + 32] if n < 3 else last_down)
            parts.append(ups_own[n])
        block = jnp.concatenate(parts, 0)
        for half in range(2):
            turned = block[:, 128 * half : 128 * half + 128].T.astype(BF)
            for b in range(8):
                y, lat = 2 * half + b // 4, b % 4
                rows = turned[16 * b : 16 * b + 16]
                for xh in range(2):
                    gt[lat % 2, z1, xh, lat // 2, y, z0] = rows[:, 128 * xh : 128 * xh + 128]


def hidden_gradient(w, chunks, weights, dq, dk, dv, acat, back, dh):
    rows = slice(WIN * w, WIN * w + WIN)
    backs = slot_lanes(back[rows, :].astype(F32), (0, 1, 2)).astype(BF)
    for c in chunks:
        cols = slice(256 * c, 256 * c + 256)
        total = dot(backs, acat[:, cols])
        for weight, d in zip(weights[:3], (dq, dk, dv)):
            total = total + dot_nt(d[rows, :], weight[cols, :])
        dh[rows, cols] = total.astype(BF)


def norm_gradient(w, w_tok, w_cot, scale, mean, rstd, dh, tg):
    gain = gain_of(scale)
    for i in range(0, WIN, 48):
        rows = slice(WIN * w + i, WIN * w + i + 48)
        inverse = rstd[rows, :]
        xhat = (w_tok[rows, :].astype(F32) - mean[rows, :]) * inverse
        g = dh[rows, :].astype(F32) * gain
        first = jnp.mean(g, axis=-1, keepdims=True)
        second = jnp.mean(g * xhat, axis=-1, keepdims=True)
        tg[i : i + 48, :] = (w_cot[rows, :].astype(F32) + inverse * (g - first - xhat * second)).astype(BF)


class Reducer:
    def __init__(self):
        lon = lax.axis_index("lon")
        lat = lax.axis_index("lat")
        y = lax.rem(lon, 4)
        z = lax.rem(lon // 4, 8)
        xh, xl, core = lon // 32, lat // 2, lax.rem(lat, 2)
        self.core, self.z = core, z
        self.mine = (xh, xl, y)

        def device(xh, z, y, xl, core):
            return ((xh * 8 + z) * 4 + y, xl * 2 + core)

        self.first = device(xh, z, y, xl, 1 - core)
        self.second = []
        for n in (10, 2, 6, 14, 9, 11, 8, 1, 3, 5, 7, 13, 15, 4, 12):
            to = lax.rem(xh + n // 8, 2), lax.rem(xl + n // 4, 2), lax.rem(y + n, 4)
            self.second.append((n - 1, to, device(to[0], z, to[2], to[1], core)))
        self.third = []
        for n in (4, 3, 5, 2, 6, 1, 7):
            to = lax.rem(z + n, 8)
            self.third.append((n - 1, to, device(xh, to, y, xl, core)))

    def partners(self):
        return [self.first] + [s[-1] for s in self.second] + [s[-1] for s in self.third]

    def start_first(self, part, gt, r1, sems):
        copy = remote(gt.at[1 - self.core, part], r1.at[part], sems.at[0, part], sems.at[1, part], self.first)
        copy.start()
        return copy

    def start_second(self, part, copy, gt, r1, s1, r2, sems):
        copy.wait()
        s1[part] = (gt[self.core, part].astype(F32) + r1[part].astype(F32)).astype(BF)
        copies = []
        for n, to, device in self.second:
            sem = 2 + 15 * part + n
            copies.append(
                remote(s1.at[part, to[0], to[1], to[2]], r2.at[part, n], sems.at[0, sem], sems.at[1, sem], device)
            )
            copies[-1].start()
        return copies

    def sum_second(self, part, copies, s1, r2, s2):
        total = s1[part, self.mine[0], self.mine[1], self.mine[2]].astype(F32)
        for copy in copies:
            copy.wait()
        for n in range(15):
            total = total + r2[part, n].astype(F32)
        s2[part] = total.astype(BF)

    def start_third(self, s2, r3, sems):
        copies = []
        for n, to, device in self.third:
            sem = 32 + n
            block = s2.at[lax.rem(to // 2, 2), lax.rem(to, 2)]
            copies.append(remote(block, r3.at[n], sems.at[0, sem], sems.at[1, sem], device))
            copies[-1].start()
        return copies

    def finish(self, copies, s2, r3, down_out, up_out, factor):
        total = s2[lax.rem(self.z // 2, 2), lax.rem(self.z, 2)].astype(F32)
        for copy in copies:
            copy.wait()
        for n in range(7):
            total = total + r3[n].astype(F32)
        total = total * factor
        total = jnp.where(self.z < 4, total[:, 0:64], total[:, 64:128])
        down_out[...] = total[:, 0:32]
        up_out[...] = total[:, 32:64]


REDUCE_SCRATCH = [
    pltpu.VMEM((2, 2, 2, 2, 4, 2, 16, 128), BF),
    pltpu.VMEM((2, 2, 2, 4, 2, 16, 128), BF),
    pltpu.VMEM((2, 2, 2, 4, 2, 16, 128), BF),
    pltpu.VMEM((2, 15, 2, 16, 128), BF),
    pltpu.VMEM((2, 2, 16, 128), BF),
    pltpu.VMEM((7, 16, 128), BF),
    pltpu.SemaphoreType.DMA((2, 39)),
]
ROWS = pltpu.VMEM((TOK, D), BF)
WIDE = pltpu.VMEM((TOK, D), F32)
SQUARE = pltpu.VMEM((D, D), BF)
RAW = pltpu.VMEM((6, 12, 4, D), BF)
PIECES = [pltpu.VMEM((2, 128, D), BF), pltpu.VMEM((2, 64, 256), BF)]
TAILS = pltpu.VMEM((2, 4, 16, 256), BF)
SEMS = pltpu.SemaphoreType.DMA((2, 4, 2))


def whole(
    sizes, factor, tok_in, cot_in, scale_in, wq_in, wk_in, wv_in, wo_in, down_in, up_in, pack_in, ends_in,
    main_back, tail_back, down_out, up_out,
    raw_tok, raw_cot, scale, wq, wk, wv, wo, acat, ups, pack_table, ends, load, wide,
    main_tok, tail_tok, main_cot, tail_cot, tails_tok, tails_cot, tails_out,
    send_tok, recv_tok, send_cot, recv_cot, send_out, recv_out,
    w_tok, w_cot, hs, q, k, v, da, at, dq, dk, dv, dh, tg_a, tg_b, low, back, mean, rstd, bias,
    gt, r1, s1, r2, s2, r3, sems,
):
    reducer = Reducer()
    partners = ring_of(sizes) + reducer.partners()
    moves = [
        (tok_in, raw_tok), (pack_in, pack_table), (cot_in, raw_cot), (ends_in, ends), (scale_in, scale),
        (down_in, acat), (up_in, ups), (wq_in, wq), (wk_in, wk), (wv_in, wv), (wo_in, wo),
    ]
    loads = [pltpu.make_async_copy(a, b, load.at[n]) for n, (a, b) in enumerate(moves)]
    for copy in loads[:3]:
        copy.start()
    start_barrier(partners)
    weights = (wq, wk, wv, wo)

    loads[0].wait()
    for copy in loads[3:]:
        copy.start()
    natural_rows(raw_tok, wide)
    loads[1].wait()
    pack(wide, pack_table, main_tok, tail_tok)
    end_barrier(partners)
    tok_copies = in_copies(sizes, main_tok, tail_tok, w_tok, tails_tok, send_tok, recv_tok)
    for copy in tok_copies:
        copy.start()
    keep_own(main_tok, tail_tok, w_tok, tails_tok)
    loads[2].wait()
    natural_rows(raw_cot, wide)
    pack(wide, pack_table, main_cot, tail_cot)
    keep_own(main_cot, tail_cot, w_cot, tails_cot)
    make_bias(sizes, bias)
    cot_copies = in_copies(sizes, main_cot, tail_cot, w_cot, tails_cot, send_cot, recv_cot)
    for copy in cot_copies[:8]:
        copy.start()
    for ahead, copy in zip(tok_copies[8:], cot_copies[8:]):
        ahead.wait_send()
        copy.start()
    for copy in loads[3:]:
        copy.wait()
    for copy in tok_copies:
        copy.wait_recv()
    for w in range(2):
        tails_to_window(ends, tails_tok[w], w_tok, WIN * w)
    norm_rows(w_tok, scale, hs, mean, rstd)
    project_tokens(hs, weights, ups, acat, low, q, k, v)
    for copy in tok_copies[:8]:
        copy.wait_send()
    for copy in cot_copies:
        copy.wait()
    for w in range(2):
        tails_to_window(ends, tails_cot[w], w_cot, WIN * w)
    project_cotangent(w_cot, wo, ups, acat, back, da)
    attend(q, k, v, da, bias, at, dq, dk, dv)
    sides = adapter_sides(w_cot, at, dq, dk, dv, ups, acat, low, back)
    first = []
    for part in range(2):
        lora_partials(part, sides, hs, w_cot, at, dq, dk, dv, gt)
        first.append(reducer.start_first(part, gt, r1, sems))
    second = []
    out = []
    for w, tg in enumerate((tg_a, tg_b)):
        for part in range(2):
            hidden_gradient(w, (2 * part, 2 * part + 1), weights, dq, dk, dv, acat, back, dh)
            if w == 0:
                second.append(reducer.start_second(part, first[part], gt, r1, s1, r2, sems))
        norm_gradient(w, w_tok, w_cot, scale, mean, rstd, dh, tg)
        tails_out[w] = window_to_tails(ends, tg[128:144, :])
        for copy in out_copies(w, sizes, tg, tails_out, main_back, tail_back, send_out, recv_out):
            copy.start()
            out.append(copy)
    return_own((tg_a, tg_b), tails_out, main_back, tail_back)
    for part in range(2):
        reducer.sum_second(part, second[part], s1, r2, s2)
    third = reducer.start_third(s2, r3, sems)
    for copy in out:
        copy.wait()
    reducer.finish(third, s2, r3, down_out, up_out, factor)


def unpack(table, main, tail, down, up, grad_out, down_out, up_out, wide):
    for ah in range(2):
        for k in range(4):
            cols = slice(256 * k, 256 * k + 256)
            wide[:, cols] = dot(table[k], jnp.concatenate([main[ah, :, cols], tail[ah]], 0))
        for a in range(3):
            for o in range(12):
                row = (12 * a + o) * 4
                grad_out[3 * ah + a, o] = wide[row : row + 4, :].astype(BF)
    down_out[...] = down[...]
    up_out[...] = up[...]


def vmem(n):
    return [pl.BlockSpec(memory_space=pltpu.VMEM)] * n


def local(
    sizes, tokens, cotangent, norm_scale_vector, query_matrix, key_matrix, value_matrix, output_matrix,
    adapter_down_maps, adapter_up_maps,
):
    pack_table, unpack_table, ends = move_tables()
    factor = float(TOK * sizes["lon"] * sizes["lat"]) ** (-0.5)
    anywhere = pl.BlockSpec(memory_space=pl.ANY)
    results = (
        jax.ShapeDtypeStruct((6, 12, 4, D), BF),
        jax.ShapeDtypeStruct((16, 32), F32),
        jax.ShapeDtypeStruct((16, 32), F32),
    )
    made = pl.pallas_call(
        functools.partial(whole, sizes, factor),
        out_shape=(
            jax.ShapeDtypeStruct((2, 128, D), BF), jax.ShapeDtypeStruct((2, 64, 256), BF), *results[1:],
        ),
        in_specs=[anywhere] * 11,
        out_specs=tuple(vmem(4)),
        scratch_shapes=[
            RAW, RAW, pltpu.VMEM((8, 128), BF), SQUARE, SQUARE, SQUARE, SQUARE,
            pltpu.VMEM((128, D), BF), pltpu.VMEM((128, D), BF),
            pltpu.VMEM((4, 192, 144), BF), pltpu.VMEM((128, 64), BF), pltpu.SemaphoreType.DMA((11,)), WIDE,
        ]
        + PIECES * 2
        + [TAILS] * 3
        + [SEMS] * 6
        + [ROWS] * 12
        + [pltpu.VMEM((WIN, D), BF)] * 2
        + [
            pltpu.VMEM((TOK, 128), BF), pltpu.VMEM((TOK, 128), BF),
            pltpu.VMEM((TOK, 1), F32), pltpu.VMEM((TOK, 1), F32), pltpu.VMEM((2, WIN, 4 * WIN), F32),
        ]
        + REDUCE_SCRATCH,
        compiler_params=pltpu.CompilerParams(
            collective_id=0, has_side_effects=True, vmem_limit_bytes=VMEM_LIMIT
        ),
    )(
        tokens.transpose(1, 2, 0, 3), cotangent.transpose(1, 2, 0, 3), norm_scale_vector.reshape(8, 128),
        query_matrix, key_matrix, value_matrix, output_matrix,
        adapter_down_maps.transpose(0, 2, 1).reshape(128, D), adapter_up_maps.reshape(128, D),
        pack_table, ends,
    )
    grad, down, up = pl.pallas_call(
        unpack,
        out_shape=results,
        in_specs=vmem(5),
        out_specs=tuple(vmem(3)),
        scratch_shapes=[pltpu.VMEM((WIN, D), F32)],
        compiler_params=pltpu.CompilerParams(vmem_limit_bytes=VMEM_LIMIT),
    )(unpack_table, *made)
    return grad.transpose(2, 0, 1, 3), down, up.T


def solution(mesh):
    sizes = dict(mesh.shape)
    spread = P(None, "lat", "lon", None)
    return jax.shard_map(
        functools.partial(local, sizes),
        mesh=mesh,
        in_specs=(spread, spread, P(), P(), P(), P(), P(), P(), P()),
        out_specs=(spread, P(("lon", "lat"), None), P(None, ("lon", "lat"))),
        check_vma=False,
    )
```
